128 devices in a mesh: ia: 8 (over z, core), ja: 4 (over x), ka: 4 (over y).
Axes of the slice: x: 4, y: 4, z: 4, core: 2. Of those that a mesh axis runs over, the one named last changes fastest.
Arguments:
- tensor: float32 [32, 128, 256, 512], P(None, 'ia', 'ja', 'ka'), may hold values from -9 to 9
- factor_b: float32 [32, 4, 64, 64], P(None, 'ja', ('ia', 'ka')), may hold values from -3 to 3
- factor_c: float32 [32, 4, 128, 64], P(None, 'ka', ('ia', 'ja')), may hold values from -3 to 3
Outputs:
- factor_a: float32 [32, 8, 16, 64], P(None, 'ia', ('ja', 'ka'))
- gram_a: float32 [32, 64, 64], replicated
The draws below stay inside these ranges and needn't reach their ends.
All inputs are finite; a program needn't handle non-finite values.
Results may differ from the reference program's by a relative error of at most 0.00045.
Values sent between devices are 32-bit elements; how exact they have to be, the bound alone decides.
No kernel may reach another device: no remote copies, remote signals or barrier semaphores. Data moves between devices by JAX's collectives and lax.ppermute only.
A program may use at most 128 MiB of HBM per device.

```python
import jax
import jax.numpy as jnp
from jax import lax

RANK = 64
FIELDS = 32
ID = 16
JD = 64
KD = 128
I = 128
J = 256
K = 512
N_IA = 8
N_JA = 4
N_KA = 4


def factor_scales(key, groups, per):
    total = groups * per
    place = (jnp.arange(groups)[:, None] * per + jnp.arange(per)[None, :]).astype(jnp.float32) / float(total - 1)
    rising = 1.0 + 2.0 * place
    key_row, key_col = jax.random.split(key)
    row_scale = jnp.exp(jax.random.uniform(key_row, (FIELDS, groups, per, 1)) * jnp.log(10.0)) * rising[None, :, :, None]
    col_scale = jnp.exp(jax.random.uniform(key_col, (FIELDS, 1, 1, RANK)) * jnp.log(3.2)) * 0.5
    return row_scale * col_scale / jnp.sqrt(93.0 * total)


def permute_columns(subkey):
    return jax.random.permutation(subkey, RANK)


def column_layout(key):
    subkeys = jax.random.split(jax.random.fold_in(key, 23), FIELDS)
    order = jax.vmap(permute_columns)(subkeys).astype(jnp.int32)
    swapped = order.reshape(FIELDS, RANK // 2, 2)[:, :, ::-1].reshape(FIELDS, RANK)
    position = jnp.argsort(order, axis=1).astype(jnp.int32)
    partner = jnp.take_along_axis(swapped, position, axis=1)
    second = position % 2 == 1
    return (partner, second)


def join_columns(values, partner, second, spread):
    index = jnp.broadcast_to(partner[:, None, None, :], values.shape)
    other = jnp.take_along_axis(values, index, axis=3)
    joined = (other + spread * values) / (1.0 + spread)
    return jnp.where(second[:, None, None, :], joined, values)


def draw_tensor(key, part):
    key = jax.random.fold_in(key, 5)
    shape = (FIELDS, I, J, K)
    place = jnp.arange(I).astype(jnp.float32) / float(I - 1)
    rising = ((1.0 + 2.0 * place) / jnp.sqrt(13.0 / 3.0))[None, :, None, None]
    base = jnp.clip(jax.random.normal(key, shape, jnp.float32), -6.0, 6.0)
    return base * rising


def draw_factor_b(key, part):
    partner, second = column_layout(key)
    key = jax.random.fold_in(key, 11)
    key_scale = jax.random.fold_in(key, 0)
    key_base = jax.random.fold_in(key, 1)
    key_spread = jax.random.fold_in(key, 3)
    shape = (FIELDS, N_JA, JD, RANK)
    spread = jnp.exp(jax.random.uniform(key_spread, (FIELDS, 1, 1, RANK), jnp.float32, jnp.log(0.06), jnp.log(0.3)))
    base = jnp.clip(jax.random.normal(key_base, shape, jnp.float32), -6.0, 6.0)
    base = join_columns(base, partner, second, spread)
    return base * factor_scales(key_scale, N_JA, JD)


def draw_factor_c(key, part):
    partner, second = column_layout(key)
    key = jax.random.fold_in(key, 17)
    key_scale = jax.random.fold_in(key, 0)
    key_base = jax.random.fold_in(key, 1)
    key_spread = jax.random.fold_in(key, 3)
    shape = (FIELDS, N_KA, KD, RANK)
    spread = jnp.exp(jax.random.uniform(key_spread, (FIELDS, 1, 1, RANK), jnp.float32, jnp.log(0.06), jnp.log(0.3)))
    base = jnp.clip(jax.random.normal(key_base, shape, jnp.float32), -6.0, 6.0)
    base = join_columns(base, partner, second, spread)
    return base * factor_scales(key_scale, N_KA, KD)


def setup_inputs(seed: int = 0) -> dict:
    streams_of = jax.random.split(jax.random.key(seed), 4)
    tensor = draw_tensor(jax.random.fold_in(streams_of[3], 71), 0)
    factor_b = draw_factor_b(jax.random.fold_in(streams_of[3], 71), 0)
    factor_c = draw_factor_c(jax.random.fold_in(streams_of[3], 71), 0)
    return {"tensor": tensor, "factor_b": factor_b, "factor_c": factor_c}


HIGH = lax.Precision.HIGHEST

def one_field(operands):
    block, rows_b, rows_c = operands
    inner = jnp.einsum('ijk,jr->rik', block, rows_b, precision=HIGH)
    return jnp.einsum('rik,kr->ir', inner, rows_c, precision=HIGH)

def solve_one(lower, rhs):
    return jax.scipy.linalg.cho_solve((lower, True), rhs.T).T

def reference(tensor, factor_b, factor_c):
    rows_b = factor_b.reshape(FIELDS, J, RANK)
    rows_c = factor_c.reshape(FIELDS, K, RANK)
    gram_b = jnp.einsum('fjr,fjs->frs', rows_b, rows_b, precision=HIGH)
    gram_c = jnp.einsum('fkr,fks->frs', rows_c, rows_c, precision=HIGH)
    mttkrp = lax.map(one_field, (tensor, rows_b, rows_c))
    lower = jax.vmap(jnp.linalg.cholesky)(gram_b * gram_c)
    rows_a = jax.vmap(solve_one)(lower, mttkrp)
    gram_a = jnp.einsum('fir,fis->frs', rows_a, rows_a, precision=HIGH) / float(I)
    return (rows_a.reshape(FIELDS, N_IA, ID, RANK), gram_a)
```

```python
import functools

import jax
import jax.numpy as jnp
from jax import lax
from jax.experimental import pallas as pl
from jax.experimental.pallas import tpu as pltpu
from jax.sharding import PartitionSpec as P

FIELDS, RANK = 32, 64
PAIRS = FIELDS // 2
ID, JD, KD = 16, 64, 128
N_IA, N_JA, N_KA = 8, 4, 4
N_Z = N_IA // 2
B_OWN = JD // (N_IA * N_KA)
C_OWN = KD // (N_IA * N_JA)
I_ALL = N_IA * ID
B_PART = JD // N_KA
C_PART = KD // N_JA
HIGH = lax.Precision.HIGHEST
MIB = 1024 * 1024
VMEM = pl.BlockSpec(memory_space=pltpu.VMEM)
ANY = pl.BlockSpec(memory_space=pl.ANY)
SLOTS = 4


def call(kernel, out_shape, operands, *, specs=None, scratch=(), vmem=16, cost=None):
    return pl.pallas_call(
        kernel,
        out_shape=out_shape,
        in_specs=[VMEM] * len(operands) if specs is None else specs,
        out_specs=jax.tree.map(lambda _: VMEM, out_shape),
        scratch_shapes=list(scratch),
        cost_estimate=cost,
        compiler_params=pltpu.CompilerParams(vmem_limit_bytes=vmem * MIB),
    )(*operands)


def f32(*shape):
    return jax.ShapeDtypeStruct(shape, jnp.float32)


def place():
    ia = lax.axis_index("ia")
    return ia // 2, lax.rem(ia, 2), lax.axis_index("ja"), lax.axis_index("ka")


def split_kernel(x_hbm, out, buffer, sems):
    def copy(f):
        slot = lax.rem(f, SLOTS)
        return pltpu.make_async_copy(x_hbm.at[f], buffer.at[slot], sems.at[slot])

    for f in range(SLOTS):
        copy(f).start()

    def step(f, carry):
        copy(f).wait()
        x = buffer[lax.rem(f, SLOTS)].reshape(ID * JD, KD)
        high = x.astype(jnp.bfloat16)
        low = (x - high.astype(jnp.float32)).astype(jnp.bfloat16)
        out[f, :, :KD] = high
        out[f, :, KD:] = low

        @pl.when(f + SLOTS < FIELDS)
        def _():
            copy(f + SLOTS).start()

        return carry

    lax.fori_loop(0, FIELDS, step, 0)


def pack_kernel(b, c, out):
    for p in range(PAIRS):
        for side in range(2):
            lanes = slice(side * RANK, (side + 1) * RANK)
            out[p, 0:B_OWN, lanes] = b[2 * p + side]
            out[p, B_OWN : B_OWN + C_OWN, lanes] = c[2 * p + side]
        out[p, B_OWN + C_OWN :, :] = jnp.zeros((8 - B_OWN - C_OWN, 2 * RANK), jnp.float32)


def in_order(pieces, first, rows):
    n = len(pieces)
    rising = jnp.concatenate([pieces[-t % n] for t in range(n)], axis=0)
    return pltpu.roll(rising, first * rows, 0)


def along_z_kernel(m0, m1, m2, m3, b, c):
    z, _, _, _ = place()
    parts = (m0, m1, m2, m3)
    for p in range(PAIRS):
        b[p] = in_order([m[p, :B_OWN, :] for m in parts], z, B_OWN)
        c[p] = in_order([m[p, B_OWN : B_OWN + C_OWN, :] for m in parts], z, C_OWN)


def along_xy_kernel(b0, b1, b2, b3, c0, c1, c2, c3, out):
    _, _, x, y = place()
    for p in range(PAIRS):
        for z in range(N_Z):
            rows = slice(z * B_OWN, (z + 1) * B_OWN)
            n = B_OWN * N_KA
            out[p, z * n : (z + 1) * n, :] = in_order([b[p, rows, :] for b in (b0, b1, b2, b3)], y, B_OWN)
        for z in range(N_Z):
            rows = slice(z * C_OWN, (z + 1) * C_OWN)
            n = C_OWN * N_JA
            at = JD // 2 + z * n
            out[p, at : at + n, :] = in_order([c[p, rows, :] for c in (c0, c1, c2, c3)], x, C_OWN)


def swap_halves(v):
    return pltpu.roll(v, RANK, 1)


def mttkrp_kernel(xs, mine, other, out, rows_b, rows_c, weights, scaled):
    _, core, x, y = place()
    lane = lax.broadcasted_iota(jnp.int32, (1, 2 * RANK), 1)
    left = lane < RANK
    nb, nc = B_OWN * N_KA, C_OWN * N_JA

    def step(p, carry):
        for z in range(N_Z):
            for source, c in ((mine, core), (other, 1 - core)):
                at = pl.multiple_of(z * 2 * nb + c * nb, nb)
                rows_b[pl.ds(at, nb), :] = source[p, z * nb : (z + 1) * nb, :]
                at = pl.multiple_of(z * 2 * nc + c * nc, nc)
                rows_c[pl.ds(at, nc), :] = source[p, JD // 2 + z * nc : JD // 2 + (z + 1) * nc, :]
        b, c = rows_b[...], rows_c[...]
        out[p, ID : ID + B_PART, :] = rows_b[pl.ds(pl.multiple_of(y * B_PART, B_PART), B_PART), :]
        out[p, ID + B_PART :, :] = rows_c[pl.ds(pl.multiple_of(x * C_PART, C_PART), C_PART), :]
        c1 = c.astype(jnp.bfloat16).astype(jnp.float32)
        c2 = (c - c1).astype(jnp.bfloat16).astype(jnp.float32)
        c3 = c - c1 - c2
        sums = []
        for side in range(2):
            if side == 0:
                first = jnp.where(left, c1, swap_halves(c2))
                second = jnp.where(left, c3, 0.0)
                weight = jnp.where(left, b, swap_halves(b))
            else:
                first = jnp.where(left, swap_halves(c1), c2)
                second = jnp.where(left, swap_halves(c3), 0.0)
                weight = jnp.where(left, swap_halves(b), b)
            for half in range(2):
                rows = slice(half * KD, (half + 1) * KD)
                weights[side, rows, :KD] = first.astype(jnp.bfloat16)
                weights[side, rows, KD:] = second.astype(jnp.bfloat16)
            product = jnp.dot(xs[2 * p + side], weights[side], preferred_element_type=jnp.float32)
            product = product.reshape(ID, JD, 4 * RANK)
            total = jnp.sum(product[:, :, :KD] * weight + product[:, :, KD:] * weight, axis=1)
            sums.append(total)
        even = sums[0] + swap_halves(sums[0])
        odd = sums[1] + swap_halves(sums[1])
        out[p, :ID, :] = jnp.where(left, even, odd)
        return carry

    lax.fori_loop(0, PAIRS, step, 0)


def total_kernel(received, out):
    total = received[0, :ID, :]
    for s in range(1, N_JA * N_KA):
        total = total + received[s, :ID, :]
    out[...] = total


def rows_gram(rows):
    return lax.dot_general(rows, rows, (((0,), (0,)), ((), ())), precision=HIGH, preferred_element_type=jnp.float32)


def factor_kernel(received, out):
    n = N_JA * N_KA
    gram = rows_gram(received[:, ID : ID + B_PART, :].reshape(n * B_PART, 2 * RANK))
    gram = gram * rows_gram(received[:, ID + B_PART :, :].reshape(n * C_PART, 2 * RANK))
    lane = lax.broadcasted_iota(jnp.int32, (RANK, 2 * RANK), 1)
    row = lax.broadcasted_iota(jnp.int32, (RANK, 2 * RANK), 0)
    eye = jnp.where(lane == row + RANK, 1.0, 0.0)
    sides = (gram[:RANK], swap_halves(gram[RANK:]))
    tiles = [[jnp.where(lane < RANK, s, eye)[8 * t : 8 * t + 8] for t in range(RANK // 8)] for s in sides]
    sub = lax.broadcasted_iota(jnp.int32, (8, 1), 0)
    for k in range(RANK):
        t, r = divmod(k, 8)
        for z in tiles:
            pivot_row = z[t][r : r + 1, :]
            step = pivot_row * (1.0 / pivot_row[:, k : k + 1])
            for u in range(t, RANK // 8):
                column = z[u][:, k : k + 1]
                if u == t:
                    if r == 7:
                        continue
                    column = jnp.where(sub > r, column, 0.0)
                z[u] = z[u] - column * step
    for side, z in enumerate(tiles):
        z = jnp.concatenate(z, axis=0)
        pivots = jnp.sum(jnp.where(lane == row, z, 0.0), axis=1, keepdims=True)
        inverse = jnp.where(lane >= RANK, z * lax.rsqrt(pivots), 0.0)
        out[side * RANK : (side + 1) * RANK, :] = inverse if side else swap_halves(inverse)


def finish_kernel(w0, w1, w2, w3, v0, v1, v2, v3, inverse, out, every, rows):
    z, core, _, _ = place()
    for parts, c in (((w0, w1, w2, w3), core), ((v0, v1, v2, v3), 1 - core)):
        for s, part in enumerate(parts):
            at = (lax.rem(z - s + N_Z, N_Z) * 2 + c) * ID
            every[pl.ds(pl.multiple_of(at, ID), ID), :] = part[...]
    inv = inverse[...]
    half = lax.dot_general(every[...], inv, (((1,), (1,)), ((), ())), precision=HIGH, preferred_element_type=jnp.float32)
    solved = jnp.dot(half, inv, precision=HIGH, preferred_element_type=jnp.float32)
    rows[...] = solved
    gram = rows_gram(solved) * (1.0 / I_ALL)
    lane = lax.broadcasted_iota(jnp.int32, (RANK, 2 * RANK), 1)
    gram = jnp.where(lane < RANK, gram[:RANK], gram[RANK:])
    own = rows[pl.ds(pl.multiple_of((z * 2 + core) * ID, ID), ID), :]
    for q in range(ID):
        out[q, :RANK, :] = gram
        out[q, RANK:, :] = jnp.broadcast_to(own[q : q + 1], (8, 2 * RANK))


def unpack_kernel(received, rows, gram):
    for p in range(PAIRS):
        for side in range(2):
            lanes = slice(side * RANK, (side + 1) * RANK)
            gram[2 * p + side] = received[p, :RANK, lanes]
            rows[2 * p + side, 0] = received[p, RANK : RANK + 1, lanes]


def shifts(n, stride=1):
    return [[(i, (i + s * stride) % (n * stride)) for i in range(n * stride)] for s in range(1, n)]


CORE_SWAP = [(i, i ^ 1) for i in range(N_IA)]


def around(value, axis, perms):
    return [value] + [lax.ppermute(value, axis, perm) for perm in perms]


def on_device(tensor, factor_b, factor_c):
    z_shifts, line = shifts(N_Z, 2), shifts(4)
    packed = call(pack_kernel, f32(PAIRS, 8, 2 * RANK), (factor_b[:, 0], factor_c[:, 0]))
    xs = call(
        split_kernel,
        pltpu.VMEM((FIELDS, ID * JD, 2 * KD), jnp.bfloat16),
        (tensor,),
        specs=[ANY],
        scratch=[pltpu.VMEM((SLOTS, ID, JD, KD), jnp.float32), pltpu.SemaphoreType.DMA((SLOTS,))],
        vmem=24,
        cost=pl.CostEstimate(flops=5 * tensor.size, bytes_accessed=4 * tensor.size, transcendentals=0),
    )
    parts = around(packed, "ia", z_shifts)
    b, c = call(along_z_kernel, (f32(PAIRS, 8, 2 * RANK), f32(PAIRS, 16, 2 * RANK)), parts)
    parts = around(b, "ka", line) + around(c, "ja", line)
    mine = call(along_xy_kernel, f32(PAIRS, 96, 2 * RANK), parts)
    other = lax.ppermute(mine, "ia", CORE_SWAP)
    sent = call(
        mttkrp_kernel,
        f32(PAIRS, ID + B_PART + C_PART, 2 * RANK),
        (xs, mine, other),
        scratch=[
            pltpu.VMEM((JD, 2 * RANK), jnp.float32),
            pltpu.VMEM((KD, 2 * RANK), jnp.float32),
            pltpu.VMEM((2, 2 * KD, 4 * RANK), jnp.bfloat16),
            pltpu.VMEM((8, 128), jnp.float32),
        ],
        vmem=40,
    )
    received = lax.all_to_all(sent, ("ja", "ka"), 0, 0)
    owned = call(total_kernel, f32(ID, 2 * RANK), (received,))
    parts = around(owned, "ia", z_shifts)
    inverse = call(
        factor_kernel,
        f32(2 * RANK, 2 * RANK),
        (received,),
        cost=pl.CostEstimate(flops=64 * 64 * 64 * 64, bytes_accessed=MIB, transcendentals=0),
    )
    parts = parts + [lax.ppermute(part, "ia", CORE_SWAP) for part in parts]
    sent = call(
        finish_kernel,
        f32(PAIRS, RANK + 8, 2 * RANK),
        (*parts, inverse),
        scratch=[pltpu.VMEM((I_ALL, 2 * RANK), jnp.float32)] * 2,
    )
    received = lax.all_to_all(sent, ("ja", "ka"), 0, 0)
    rows, gram = call(unpack_kernel, (f32(FIELDS, 1, 1, RANK), f32(FIELDS, RANK, RANK)), (received,))
    return rows, gram


def solution(mesh):
    return jax.shard_map(
        on_device,
        mesh=mesh,
        in_specs=(
            P(None, "ia", "ja", "ka"),
            P(None, "ja", ("ia", "ka"), None),
            P(None, "ka", ("ia", "ja"), None),
        ),
        out_specs=(P(None, "ia", ("ja", "ka"), None), P()),
        check_vma=False,
    )
```

```python
import functools

import jax
import jax.numpy as jnp
from jax import lax
from jax.experimental import pallas as pl
from jax.experimental.pallas import tpu as pltpu
from jax.sharding import PartitionSpec as P

FIELDS, RANK = 32, 64
PAIRS = FIELDS // 2
ID, JD, KD = 16, 64, 128
N_IA, N_JA, N_KA = 8, 4, 4
N_Z = N_IA // 2
B_OWN = JD // (N_IA * N_KA)
C_OWN = KD // (N_IA * N_JA)
I_ALL = N_IA * ID
B_PART = JD // N_KA
C_PART = KD // N_JA
HIGH = lax.Precision.HIGHEST
MIB = 1024 * 1024
VMEM = pl.BlockSpec(memory_space=pltpu.VMEM)
ANY = pl.BlockSpec(memory_space=pl.ANY)
UNROLL = 4


def call(kernel, out_shape, operands, *, specs=None, scratch=(), vmem=16, cost=None):
    return pl.pallas_call(
        kernel,
        out_shape=out_shape,
        in_specs=[VMEM] * len(operands) if specs is None else specs,
        out_specs=jax.tree.map(lambda _: VMEM, out_shape),
        scratch_shapes=list(scratch),
        cost_estimate=cost,
        compiler_params=pltpu.CompilerParams(vmem_limit_bytes=vmem * MIB),
    )(*operands)


def f32(*shape):
    return jax.ShapeDtypeStruct(shape, jnp.float32)


def place():
    ia = lax.axis_index("ia")
    return ia // 2, lax.rem(ia, 2), lax.axis_index("ja"), lax.axis_index("ka")


def pack_kernel(b_hbm, c_hbm, tensor, out, b, c, sems):
    copies = [pltpu.make_async_copy(b_hbm, b, sems.at[0]), pltpu.make_async_copy(c_hbm, c, sems.at[1])]
    for copy in copies:
        copy.start()
    for copy in copies:
        copy.wait()
    for p in range(PAIRS):
        for side in range(2):
            lanes = slice(side * RANK, (side + 1) * RANK)
            out[p, 0:B_OWN, lanes] = b[2 * p + side]
            out[p, B_OWN : B_OWN + C_OWN, lanes] = c[2 * p + side]
        out[p, B_OWN + C_OWN :, :] = jnp.zeros((8 - B_OWN - C_OWN, 2 * RANK), jnp.float32)


def in_order(pieces, first, rows):
    n = len(pieces)
    rising = jnp.concatenate([pieces[-t % n] for t in range(n)], axis=0)
    return pltpu.roll(rising, first * rows, 0)


def along_z_kernel(m0, m1, m2, m3, b, c):
    z, _, _, _ = place()
    parts = (m0, m1, m2, m3)
    for p in range(PAIRS):
        b[p] = in_order([m[p, :B_OWN, :] for m in parts], z, B_OWN)
        c[p] = in_order([m[p, B_OWN : B_OWN + C_OWN, :] for m in parts], z, C_OWN)


def along_xy_kernel(b0, b1, b2, b3, c0, c1, c2, c3, out):
    _, _, x, y = place()
    for p in range(PAIRS):
        for z in range(N_Z):
            rows = slice(z * B_OWN, (z + 1) * B_OWN)
            n = B_OWN * N_KA
            out[p, z * n : (z + 1) * n, :] = in_order([b[p, rows, :] for b in (b0, b1, b2, b3)], y, B_OWN)
        for z in range(N_Z):
            rows = slice(z * C_OWN, (z + 1) * C_OWN)
            n = C_OWN * N_JA
            at = JD // 2 + z * n
            out[p, at : at + n, :] = in_order([c[p, rows, :] for c in (c0, c1, c2, c3)], x, C_OWN)


def swap_halves(v):
    return pltpu.roll(v, RANK, 1)


def mttkrp_kernel(tensor, mine, other, out):
    _, core, x, y = place()
    lane = lax.broadcasted_iota(jnp.int32, (1, 2 * RANK), 1)
    left = lane < RANK
    first_core = core == 0
    nb, nc = B_OWN * N_KA, C_OWN * N_JA

    def both(p, at, rows):
        here, there = mine[p, pl.ds(at, rows), :], other[p, pl.ds(at, rows), :]
        return [jnp.where(first_core, here, there), jnp.where(first_core, there, here)]

    def pair(p):
        b = jnp.concatenate([part for z in range(N_Z) for part in both(p, z * nb, nb)], axis=0)
        c = jnp.concatenate([part for z in range(N_Z) for part in both(p, JD // 2 + z * nc, nc)], axis=0)
        out[p, ID : ID + B_PART, :] = jnp.concatenate(both(p, pl.multiple_of(y * nb, nb), nb), axis=0)
        out[p, ID + B_PART :, :] = jnp.concatenate(both(p, pl.multiple_of(JD // 2 + x * nc, nc), nc), axis=0)
        c1 = c.astype(jnp.bfloat16).astype(jnp.float32)
        c2 = (c - c1).astype(jnp.bfloat16).astype(jnp.float32)
        c3 = c - c1 - c2
        sums = []
        for side in range(2):
            if side == 0:
                first = jnp.where(left, c1, swap_halves(c2))
                second = jnp.where(left, c3, 0.0)
                weight = jnp.where(left, b, swap_halves(b))
            else:
                first = jnp.where(left, swap_halves(c1), c2)
                second = jnp.where(left, swap_halves(c3), 0.0)
                weight = jnp.where(left, swap_halves(b), b)
            pieces = jnp.concatenate([first.astype(jnp.bfloat16), second.astype(jnp.bfloat16)], axis=1)
            block = tensor[2 * p + side].reshape(ID * JD, KD)
            high = block.astype(jnp.bfloat16)
            low = (block - high.astype(jnp.float32)).astype(jnp.bfloat16)
            product = jnp.dot(
                jnp.concatenate([high, low], axis=1),
                jnp.concatenate([pieces, pieces], axis=0),
                preferred_element_type=jnp.float32,
            )
            product = (product[:, :KD] + product[:, KD:]).reshape(ID, JD, KD) * weight
            sums.append(jnp.sum(product.reshape(ID, JD // 8, 8, KD).sum(axis=1), axis=1))
        even = sums[0] + swap_halves(sums[0])
        odd = sums[1] + swap_halves(sums[1])
        out[p, :ID, :] = jnp.where(left, even, odd)

    def step(n, carry):
        for u in range(UNROLL):
            pair(n * UNROLL + u)
        return carry

    lax.fori_loop(0, PAIRS // UNROLL, step, 0)


def total_kernel(received, out):
    total = received[0, :ID, :]
    for s in range(1, N_JA * N_KA):
        total = total + received[s, :ID, :]
    out[...] = total


def rows_gram(rows):
    return lax.dot_general(rows, rows, (((0,), (0,)), ((), ())), precision=HIGH, preferred_element_type=jnp.float32)


def factor_kernel(received, out):
    n = N_JA * N_KA
    gram = rows_gram(received[:, ID : ID + B_PART, :].reshape(n * B_PART, 2 * RANK))
    gram = gram * rows_gram(received[:, ID + B_PART :, :].reshape(n * C_PART, 2 * RANK))
    lane = lax.broadcasted_iota(jnp.int32, (RANK, 2 * RANK), 1)
    row = lax.broadcasted_iota(jnp.int32, (RANK, 2 * RANK), 0)
    eye = jnp.where(lane == row + RANK, 1.0, 0.0)
    sides = (gram[:RANK], swap_halves(gram[RANK:]))
    tiles = [[jnp.where(lane < RANK, s, eye)[8 * t : 8 * t + 8] for t in range(RANK // 8)] for s in sides]
    sub = lax.broadcasted_iota(jnp.int32, (8, 1), 0)
    for k in range(RANK):
        t, r = divmod(k, 8)
        for z in tiles:
            pivot_row = z[t][r : r + 1, :]
            step = pivot_row * (1.0 / pivot_row[:, k : k + 1])
            for u in range(t, RANK // 8):
                column = z[u][:, k : k + 1]
                if u == t:
                    if r == 7:
                        continue
                    column = jnp.where(sub > r, column, 0.0)
                z[u] = z[u] - column * step
    for side, z in enumerate(tiles):
        z = jnp.concatenate(z, axis=0)
        pivots = jnp.sum(jnp.where(lane == row, z, 0.0), axis=1, keepdims=True)
        inverse = jnp.where(lane >= RANK, z * lax.rsqrt(pivots), 0.0)
        out[side * RANK : (side + 1) * RANK, :] = inverse if side else swap_halves(inverse)


def finish_kernel(w0, w1, w2, w3, v0, v1, v2, v3, inverse, out, every, rows):
    z, core, _, _ = place()
    for parts, c in (((w0, w1, w2, w3), core), ((v0, v1, v2, v3), 1 - core)):
        for s, part in enumerate(parts):
            at = (lax.rem(z - s + N_Z, N_Z) * 2 + c) * ID
            every[pl.ds(pl.multiple_of(at, ID), ID), :] = part[...]
    inv = inverse[...]
    half = lax.dot_general(every[...], inv, (((1,), (1,)), ((), ())), precision=HIGH, preferred_element_type=jnp.float32)
    solved = jnp.dot(half, inv, precision=HIGH, preferred_element_type=jnp.float32)
    rows[...] = solved
    gram = rows_gram(solved) * (1.0 / I_ALL)
    lane = lax.broadcasted_iota(jnp.int32, (RANK, 2 * RANK), 1)
    gram = jnp.where(lane < RANK, gram[:RANK], gram[RANK:])
    own = rows[pl.ds(pl.multiple_of((z * 2 + core) * ID, ID), ID), :]
    for q in range(ID):
        out[q, :RANK, :] = gram
        out[q, RANK:, :] = jnp.broadcast_to(own[q : q + 1], (8, 2 * RANK))


def unpack_kernel(received, rows, gram):
    for p in range(PAIRS):
        for side in range(2):
            lanes = slice(side * RANK, (side + 1) * RANK)
            gram[2 * p + side] = received[p, :RANK, lanes]
            rows[2 * p + side, 0] = received[p, RANK : RANK + 1, lanes]


def shifts(n, stride=1):
    return [[(i, (i + s * stride) % (n * stride)) for i in range(n * stride)] for s in range(1, n)]


CORE_SWAP = [(i, i ^ 1) for i in range(N_IA)]


def around(value, axis, perms):
    return [value] + [lax.ppermute(value, axis, perm) for perm in perms]


def on_device(tensor, factor_b, factor_c):
    z_shifts, line = shifts(N_Z, 2), shifts(4)
    packed = call(
        pack_kernel,
        f32(PAIRS, 8, 2 * RANK),
        [pltpu.with_memory_space_constraint(f, pltpu.HBM) for f in (factor_b[:, 0], factor_c[:, 0], tensor)],
        specs=[ANY, ANY, ANY],
        scratch=[
            pltpu.VMEM((FIELDS, B_OWN, RANK), jnp.float32),
            pltpu.VMEM((FIELDS, C_OWN, RANK), jnp.float32),
            pltpu.SemaphoreType.DMA((2,)),
        ],
    )
    parts = around(packed, "ia", z_shifts)
    near = pltpu.with_memory_space_constraint(tensor, pltpu.VMEM)
    b, c = call(along_z_kernel, (f32(PAIRS, 8, 2 * RANK), f32(PAIRS, 16, 2 * RANK)), parts)
    parts = around(b, "ka", line) + around(c, "ja", line)
    mine = call(along_xy_kernel, f32(PAIRS, 96, 2 * RANK), parts)
    other = lax.ppermute(mine, "ia", CORE_SWAP)
    sent = call(
        mttkrp_kernel,
        f32(PAIRS, ID + B_PART + C_PART, 2 * RANK),
        (near, mine, other),
        vmem=28,
        cost=pl.CostEstimate(flops=8 * 2 * tensor.size * RANK, bytes_accessed=4 * tensor.size, transcendentals=0),
    )
    received = lax.all_to_all(sent, ("ja", "ka"), 0, 0)
    owned = call(total_kernel, f32(ID, 2 * RANK), (received,))
    parts = around(owned, "ia", z_shifts)
    inverse = call(
        factor_kernel,
        f32(2 * RANK, 2 * RANK),
        (received,),
        cost=pl.CostEstimate(flops=4 * RANK**3, bytes_accessed=20 * MIB, transcendentals=0),
    )
    *parts, inverse = lax.optimization_barrier((*parts, inverse))
    parts = parts + [lax.ppermute(part, "ia", CORE_SWAP) for part in parts]
    sent = call(
        finish_kernel,
        f32(PAIRS, RANK + 8, 2 * RANK),
        (*parts, inverse),
        scratch=[pltpu.VMEM((I_ALL, 2 * RANK), jnp.float32)] * 2,
    )
    received = lax.all_to_all(sent, ("ja", "ka"), 0, 0)
    rows, gram = call(unpack_kernel, (f32(FIELDS, 1, 1, RANK), f32(FIELDS, RANK, RANK)), (received,))
    return rows, gram


def solution(mesh):
    return jax.shard_map(
        on_device,
        mesh=mesh,
        in_specs=(
            P(None, "ia", "ja", "ka"),
            P(None, "ja", ("ia", "ka"), None),
            P(None, "ka", ("ia", "ja"), None),
        ),
        out_specs=(P(None, "ia", ("ja", "ka"), None), P()),
        check_vma=False,
    )
```

```python
import jax
import jax.numpy as jnp
from jax import lax
from jax.experimental import pallas as pl
from jax.experimental.pallas import tpu as pltpu
from jax.sharding import Mesh
from jax.sharding import PartitionSpec as P

FIELDS, RANK = 32, 64
PAIRS = FIELDS // 2
ID, JD, KD = 16, 64, 128
N_IA, N_JA, N_KA = 8, 4, 4
N_Z = N_IA // 2
B_OWN = JD // (N_IA * N_KA)
C_OWN = KD // (N_IA * N_JA)
I_ALL = N_IA * ID
OWNERS = PAIRS * 2
HIGH = lax.Precision.HIGHEST
MIB = 1024 * 1024
VMEM = pl.BlockSpec(memory_space=pltpu.VMEM)
ANY = pl.BlockSpec(memory_space=pl.ANY)
PANEL = 16
UNROLL = 4


def call(kernel, out_shape, operands, *, specs=None, scratch=(), vmem=16, cost=None):
    return pl.pallas_call(
        kernel,
        out_shape=out_shape,
        in_specs=[VMEM] * len(operands) if specs is None else specs,
        out_specs=jax.tree.map(lambda _: VMEM, out_shape),
        scratch_shapes=list(scratch),
        cost_estimate=cost,
        compiler_params=pltpu.CompilerParams(vmem_limit_bytes=vmem * MIB),
    )(*operands)


def f32(*shape):
    return jax.ShapeDtypeStruct(shape, jnp.float32)


def place():
    return tuple(lax.axis_index(axis) for axis in ("z", "core", "ja", "ka"))


def pack_kernel(b_hbm, c_hbm, tensor, out, b, c, sems):
    copies = [pltpu.make_async_copy(b_hbm, b, sems.at[0]), pltpu.make_async_copy(c_hbm, c, sems.at[1])]
    for copy in copies:
        copy.start()
    for copy in copies:
        copy.wait()
    for p in range(PAIRS):
        for side in range(2):
            lanes = slice(side * RANK, (side + 1) * RANK)
            out[p, 0:B_OWN, lanes] = b[2 * p + side]
            out[p, B_OWN : B_OWN + C_OWN, lanes] = c[2 * p + side]
        out[p, B_OWN + C_OWN :, :] = jnp.zeros((8 - B_OWN - C_OWN, 2 * RANK), jnp.float32)


def in_order(pieces, first, rows):
    n = len(pieces)
    rising = jnp.concatenate([pieces[-t % n] for t in range(n)], axis=0)
    return pltpu.roll(rising, first * rows, 0)


def swap_halves(v):
    return pltpu.roll(v, RANK, 1)


def fold(v):
    half = v.shape[0] // 2
    lane = lax.broadcasted_iota(jnp.int32, (1, 2 * RANK), 1)
    return jnp.where(lane < RANK, v[:half], swap_halves(v[half:]))


def along_z_kernel(m0, m1, m2, m3, b, c):
    z, _, _, _ = place()
    parts = (m0, m1, m2, m3)
    for p in range(PAIRS):
        b[p] = in_order([m[p, :B_OWN, :] for m in parts], z, B_OWN)
        c[p] = in_order([m[p, B_OWN : B_OWN + C_OWN, :] for m in parts], z, C_OWN)


def along_xy_kernel(b0, b1, b2, b3, c0, c1, c2, c3, out):
    _, _, x, y = place()
    for p in range(PAIRS):
        for z in range(N_Z):
            rows = slice(z * B_OWN, (z + 1) * B_OWN)
            n = B_OWN * N_KA
            out[p, z * n : (z + 1) * n, :] = in_order([b[p, rows, :] for b in (b0, b1, b2, b3)], y, B_OWN)
        for z in range(N_Z):
            rows = slice(z * C_OWN, (z + 1) * C_OWN)
            n = C_OWN * N_JA
            at = JD // 2 + z * n
            out[p, at : at + n, :] = in_order([c[p, rows, :] for c in (c0, c1, c2, c3)], x, C_OWN)


def mttkrp_kernel(tensor, mine, other, out):
    _, core, x, y = place()
    lane = lax.broadcasted_iota(jnp.int32, (1, 2 * RANK), 1)
    left = lane < RANK
    first_core = core == 0
    nb, nc = B_OWN * N_KA, C_OWN * N_JA

    def both(p, at, rows):
        here, there = mine[p, pl.ds(at, rows), :], other[p, pl.ds(at, rows), :]
        return [jnp.where(first_core, here, there), jnp.where(first_core, there, here)]

    def pair(p):
        b = jnp.concatenate([part for z in range(N_Z) for part in both(p, z * nb, nb)], axis=0)
        c = jnp.concatenate([part for z in range(N_Z) for part in both(p, JD // 2 + z * nc, nc)], axis=0)
        part_b = mine[p, pl.ds(pl.multiple_of(y * nb, nb), nb), :]
        part_c = mine[p, pl.ds(pl.multiple_of(JD // 2 + x * nc, nc), nc), :]
        for side in range(2):
            d = side * PAIRS + p
            out[d, 8:16, :] = fold(swap_halves(part_c) if side else part_c)
            part = fold(swap_halves(part_b) if side else part_b)
            out[d, 16:24, :] = jnp.concatenate([part, jnp.zeros_like(part)], axis=0)
        c1 = c.astype(jnp.bfloat16).astype(jnp.float32)
        c2 = (c - c1).astype(jnp.bfloat16).astype(jnp.float32)
        c3 = c - c1 - c2
        for side in range(2):
            if side == 0:
                first = jnp.where(left, c1, swap_halves(c2))
                second = jnp.where(left, c3, 0.0)
                weight = jnp.where(left, b, swap_halves(b))
            else:
                first = jnp.where(left, swap_halves(c1), c2)
                second = jnp.where(left, swap_halves(c3), 0.0)
                weight = jnp.where(left, swap_halves(b), b)
            pieces = jnp.concatenate([first.astype(jnp.bfloat16), second.astype(jnp.bfloat16)], axis=1)
            block = tensor[2 * p + side].reshape(ID * JD, KD)
            high = block.astype(jnp.bfloat16)
            low = (block - high.astype(jnp.float32)).astype(jnp.bfloat16)
            product = jnp.dot(
                jnp.concatenate([high, low], axis=1),
                jnp.concatenate([pieces, pieces], axis=0),
                preferred_element_type=jnp.float32,
            )
            product = (product[:, :KD] + product[:, KD:]).reshape(ID, JD, KD) * weight
            total = jnp.sum(product.reshape(ID, JD // 8, 8, KD).sum(axis=1), axis=1)
            out[side * PAIRS + p, :8, :] = fold(total + swap_halves(total))

    def step(n, carry):
        for u in range(UNROLL):
            pair(n * UNROLL + u)
        return carry

    lax.fori_loop(0, PAIRS // UNROLL, step, 0)


def total_kernel(received, out):
    for core in range(2):
        total = received[core * PAIRS, :8, :]
        for s in range(1, PAIRS):
            total = total + received[core * PAIRS + s, :8, :]
        out[8 * core : 8 * core + 8, :] = total


def rows_gram(rows):
    both = lax.dot_general(rows, rows, (((0,), (0,)), ((), ())), precision=HIGH, preferred_element_type=jnp.float32)
    return both[:RANK] + swap_halves(both[RANK:])


def factor_kernel(received, out):
    gram = rows_gram(received[:, 16:20, :].reshape(OWNERS * 4, 2 * RANK))
    gram = gram * rows_gram(received[:, 8:16, :].reshape(OWNERS * 8, 2 * RANK))
    lane = lax.broadcasted_iota(jnp.int32, (RANK, 2 * RANK), 1)
    row = lax.broadcasted_iota(jnp.int32, (RANK, 2 * RANK), 0)
    whole = jnp.where(lane < RANK, gram, jnp.where(lane == row + RANK, 1.0, 0.0))
    n = RANK // PANEL
    panels = [whole[PANEL * t : PANEL * (t + 1)] for t in range(n)]
    sub = lax.broadcasted_iota(jnp.int32, (PANEL, 2 * RANK), 0)
    for t in range(n):
        panel = panels[t]
        columns = [
            jnp.broadcast_to(panel[:, PANEL * t + j : PANEL * t + j + 1], panel.shape) for j in range(PANEL)
        ]
        inverses = []
        for k in range(PANEL):
            inverses.append(1.0 / columns[k][k : k + 1, :])
            if k == PANEL - 1:
                break
            first = (k + 1) // 8 * 8
            factor = jnp.where(sub[first:] > k, columns[k][first:], 0.0) * inverses[k]

            def eliminate(v):
                low = v[first:] - factor * v[k : k + 1, :]
                return jnp.concatenate([v[:first], low], axis=0) if first else low

            for j in range(k + 1, PANEL):
                columns[j] = eliminate(columns[j])
            panel = eliminate(panel)
        panels[t] = panel
        if t < n - 1:
            factors = jnp.transpose(panel * jnp.concatenate(inverses, axis=0))
            for u in range(t + 1, n):
                rest = panels[u]
                for k in range(PANEL):
                    rest = rest - factors[PANEL * u : PANEL * (u + 1), k : k + 1] * panel[k : k + 1, :]
                panels[u] = rest
    whole = jnp.concatenate(panels, axis=0)
    pivots = jnp.sum(jnp.where(lane == row, whole, 0.0), axis=1, keepdims=True)
    inverse = jnp.where(lane >= RANK, whole * lax.rsqrt(pivots), 0.0)
    out[:RANK, :] = swap_halves(inverse)
    out[RANK:, :] = inverse


def finish_kernel(w0, w1, w2, w3, inverse, out, every, rows):
    z, _, _, _ = place()
    for s, part in enumerate((w0, w1, w2, w3)):
        at = lax.rem(z - s + N_Z, N_Z) * 16
        every[pl.ds(pl.multiple_of(at, 16), 16), :] = part[...]
    inv = inverse[...]
    half = lax.dot_general(every[...], inv, (((1,), (1,)), ((), ())), precision=HIGH, preferred_element_type=jnp.float32)
    solved = jnp.dot(half, inv, precision=HIGH, preferred_element_type=jnp.float32)
    rows[...] = solved
    gram = fold(rows_gram(solved) * (1.0 / I_ALL))
    own = rows[pl.ds(pl.multiple_of(z * 16, 16), 16), :]
    for core in range(2):
        for q in range(ID):
            out[core * PAIRS + q, : RANK // 2, :] = gram
            row = core * 8 + q % 8
            out[core * PAIRS + q, RANK // 2 :, :] = jnp.broadcast_to(own[row : row + 1], (8, 2 * RANK))


def unpack_kernel(received, rows, gram):
    _, _, x, y = place()
    upper = x * N_KA + y >= 8
    half = RANK // 2
    for p in range(PAIRS):
        for side in range(2):
            source = side * PAIRS + p
            gram[2 * p + side, :half] = received[source, :half, :RANK]
            gram[2 * p + side, half:] = received[source, :half, RANK:]
            row = received[source, half : half + 1, :]
            rows[2 * p + side, 0] = jnp.where(upper, row[:, RANK:], row[:, :RANK])


LINE = [[(i, (i + s) % 4) for i in range(4)] for s in range(1, 4)]


def around(value, axis):
    return [value] + [lax.ppermute(value, axis, perm) for perm in LINE]


def on_device(tensor, factor_b, factor_c):
    packed = call(
        pack_kernel,
        f32(PAIRS, 8, 2 * RANK),
        [pltpu.with_memory_space_constraint(f, pltpu.HBM) for f in (factor_b[:, 0], factor_c[:, 0], tensor)],
        specs=[ANY, ANY, ANY],
        scratch=[
            pltpu.VMEM((FIELDS, B_OWN, RANK), jnp.float32),
            pltpu.VMEM((FIELDS, C_OWN, RANK), jnp.float32),
            pltpu.SemaphoreType.DMA((2,)),
        ],
    )
    parts = around(packed, "z")
    near = pltpu.with_memory_space_constraint(tensor, pltpu.VMEM)
    b, c = call(along_z_kernel, (f32(PAIRS, 8, 2 * RANK), f32(PAIRS, 16, 2 * RANK)), parts)
    parts = around(b, "ka") + around(c, "ja")
    mine = call(along_xy_kernel, f32(PAIRS, 96, 2 * RANK), parts)
    other = lax.ppermute(mine, "core", [(0, 1), (1, 0)])
    sent = call(
        mttkrp_kernel,
        f32(OWNERS, 24, 2 * RANK),
        (near, mine, other),
        vmem=28,
        cost=pl.CostEstimate(flops=8 * 2 * tensor.size * RANK, bytes_accessed=4 * tensor.size, transcendentals=0),
    )
    received = lax.all_to_all(sent, ("core", "ja", "ka"), 0, 0)
    owned = call(total_kernel, f32(16, 2 * RANK), (received,))
    parts = around(owned, "z")
    inverse = call(
        factor_kernel,
        f32(2 * RANK, 2 * RANK),
        (received,),
        cost=pl.CostEstimate(flops=4 * RANK**3, bytes_accessed=10 * MIB, transcendentals=0),
    )
    sent = call(
        finish_kernel,
        f32(OWNERS, RANK // 2 + 8, 2 * RANK),
        (*parts, inverse),
        scratch=[pltpu.VMEM((I_ALL // 2, 2 * RANK), jnp.float32)] * 2,
    )
    received = lax.all_to_all(sent, ("core", "ja", "ka"), 0, 0)
    rows, gram = call(unpack_kernel, (f32(FIELDS, 1, 1, RANK), f32(FIELDS, RANK, RANK)), (received,))
    return rows, gram


def solution(mesh):
    return jax.shard_map(
        on_device,
        mesh=Mesh(mesh.devices.reshape(N_Z, 2, N_JA, N_KA), ("z", "core", "ja", "ka")),
        in_specs=(
            P(None, ("z", "core"), "ja", "ka"),
            P(None, "ja", ("z", "core", "ka"), None),
            P(None, "ka", ("z", "core", "ja"), None),
        ),
        out_specs=(P(None, ("z", "core"), ("ja", "ka"), None), P()),
        check_vma=False,
    )
```

```python
import jax
import jax.numpy as jnp
from jax import lax
from jax.experimental import pallas as pl
from jax.experimental.pallas import tpu as pltpu
from jax.sharding import Mesh
from jax.sharding import PartitionSpec as P

FIELDS, RANK = 32, 64
PAIRS = FIELDS // 2
ID, JD, KD = 16, 64, 128
N_IA, N_JA, N_KA = 8, 4, 4
N_Z = N_IA // 2
B_OWN = JD // (N_IA * N_KA)
C_OWN = KD // (N_IA * N_JA)
I_ALL = N_IA * ID
HIGH = lax.Precision.HIGHEST
MIB = 1024 * 1024
VMEM = pl.BlockSpec(memory_space=pltpu.VMEM)
ANY = pl.BlockSpec(memory_space=pl.ANY)
PANEL = 16
UNROLL = 8


def call(kernel, out_shape, operands, *, specs=None, scratch=(), vmem=16, cost=None):
    return pl.pallas_call(
        kernel,
        out_shape=out_shape,
        in_specs=[VMEM] * len(operands) if specs is None else specs,
        out_specs=jax.tree.map(lambda _: VMEM, out_shape),
        scratch_shapes=list(scratch),
        cost_estimate=cost,
        compiler_params=pltpu.CompilerParams(vmem_limit_bytes=vmem * MIB),
    )(*operands)


def f32(*shape):
    return jax.ShapeDtypeStruct(shape, jnp.float32)


def place():
    return tuple(lax.axis_index(axis) for axis in ("z", "core", "ja", "ka"))


def pack_kernel(b_hbm, c_hbm, tensor, out, b, c, sems):
    copies = [pltpu.make_async_copy(b_hbm, b, sems.at[0]), pltpu.make_async_copy(c_hbm, c, sems.at[1])]
    for copy in copies:
        copy.start()
    for copy in copies:
        copy.wait()
    for p in range(PAIRS):
        for side in range(2):
            lanes = slice(side * RANK, (side + 1) * RANK)
            out[p, 0:B_OWN, lanes] = b[2 * p + side]
            out[p, B_OWN : B_OWN + C_OWN, lanes] = c[2 * p + side]
        out[p, B_OWN + C_OWN :, :] = jnp.zeros((8 - B_OWN - C_OWN, 2 * RANK), jnp.float32)


def in_order(pieces, first, rows):
    n = len(pieces)
    rising = jnp.concatenate([pieces[-t % n] for t in range(n)], axis=0)
    return pltpu.roll(rising, first * rows, 0)


def swap_halves(v):
    return pltpu.roll(v, RANK, 1)


def fold(v):
    half = v.shape[0] // 2
    lane = lax.broadcasted_iota(jnp.int32, (1, 2 * RANK), 1)
    return jnp.where(lane < RANK, v[:half], swap_halves(v[half:]))


def along_z_kernel(m0, m1, m2, m3, b, c):
    z, _, _, _ = place()
    parts = (m0, m1, m2, m3)
    for p in range(PAIRS):
        b[p] = in_order([m[p, :B_OWN, :] for m in parts], z, B_OWN)
        c[p] = in_order([m[p, B_OWN : B_OWN + C_OWN, :] for m in parts], z, C_OWN)


def along_xy_kernel(b0, b1, b2, b3, c0, c1, c2, c3, out):
    _, _, x, y = place()
    for p in range(PAIRS):
        for z in range(N_Z):
            rows = slice(z * B_OWN, (z + 1) * B_OWN)
            n = B_OWN * N_KA
            out[p, z * n : (z + 1) * n, :] = in_order([b[p, rows, :] for b in (b0, b1, b2, b3)], y, B_OWN)
        for z in range(N_Z):
            rows = slice(z * C_OWN, (z + 1) * C_OWN)
            n = C_OWN * N_JA
            at = JD // 2 + z * n
            out[p, at : at + n, :] = in_order([c[p, rows, :] for c in (c0, c1, c2, c3)], x, C_OWN)


def contract(p, side, tensor, mine, other):
    first_core = lax.axis_index("core") == 0
    left = lax.broadcasted_iota(jnp.int32, (1, 2 * RANK), 1) < RANK
    nb, nc = B_OWN * N_KA, C_OWN * N_JA

    def both(at, rows):
        here, there = mine[p, at : at + rows, :], other[p, at : at + rows, :]
        return [jnp.where(first_core, here, there), jnp.where(first_core, there, here)]

    def chosen(v):
        return jnp.where(side == 0, v, swap_halves(v))

    b = chosen(jnp.concatenate([part for z in range(N_Z) for part in both(z * nb, nb)], axis=0))
    c = chosen(jnp.concatenate([part for z in range(N_Z) for part in both(JD // 2 + z * nc, nc)], axis=0))
    c1 = c.astype(jnp.bfloat16).astype(jnp.float32)
    c2 = (c - c1).astype(jnp.bfloat16).astype(jnp.float32)
    c3 = c - c1 - c2
    first = jnp.where(left, c1, swap_halves(c2))
    second = jnp.where(left, c3, 0.0)
    weight = jnp.where(left, b, swap_halves(b))
    pieces = jnp.concatenate([first.astype(jnp.bfloat16), second.astype(jnp.bfloat16)], axis=1)
    block = tensor[2 * p + side].reshape(ID * JD, KD)
    high = block.astype(jnp.bfloat16)
    low = (block - high.astype(jnp.float32)).astype(jnp.bfloat16)
    product = jnp.dot(
        jnp.concatenate([high, low], axis=1),
        jnp.concatenate([pieces, pieces], axis=0),
        preferred_element_type=jnp.float32,
    )
    product = (product[:, :KD] + product[:, KD:]).reshape(ID, JD, KD) * weight
    total = jnp.sum(product.reshape(ID, JD // 8, 8, KD).sum(axis=1), axis=1)
    return fold(total + swap_halves(total))


def by_pairs(body):
    def step(n, carry):
        for u in range(UNROLL):
            body(n * UNROLL + u)
        return carry

    lax.fori_loop(0, PAIRS // UNROLL, step, 0)


def other_fields_kernel(tensor, mine, other, out):
    side = 1 - lax.axis_index("core")

    def pair(p):
        out[p] = contract(p, side, tensor, mine, other)

    by_pairs(pair)


def own_fields_kernel(tensor, mine, other, out):
    _, core, x, y = place()
    first_core = core == 0
    nb, nc = B_OWN * N_KA, C_OWN * N_JA

    def share(p, at, rows):
        here, there = mine[p, pl.ds(at, rows), :], other[p, pl.ds(at, rows), :]
        parts = [jnp.where(first_core, here, there), jnp.where(first_core, there, here)]
        part = jnp.concatenate(parts, axis=0)
        return fold(jnp.where(first_core, part, swap_halves(part)))

    def pair(p):
        out[p, pl.ds(pl.multiple_of(8 * (1 - core), 8), 8), :] = jnp.zeros((8, 2 * RANK), jnp.float32)
        out[p, pl.ds(pl.multiple_of(8 * core, 8), 8), :] = contract(p, core, tensor, mine, other)
        out[p, 16:24, :] = share(p, pl.multiple_of(y * nb, nb), nb)
        out[p, 24:40, :] = share(p, pl.multiple_of(JD // 2 + x * nc, nc), nc)

    by_pairs(pair)


def join_kernel(sums, swapped, out):
    at = pl.multiple_of(8 * (1 - lax.axis_index("core")), 8)
    out[...] = sums[...]
    out[:, pl.ds(at, 8), :] = swapped[...]


def total_kernel(received, out):
    total = received[0, :16, :]
    for s in range(1, PAIRS):
        total = total + received[s, :16, :]
    out[...] = total


def rows_gram(rows):
    both = lax.dot_general(rows, rows, (((0,), (0,)), ((), ())), precision=HIGH, preferred_element_type=jnp.float32)
    return both[:RANK] + swap_halves(both[RANK:])


def factor_kernel(received, out):
    gram = rows_gram(received[:, 16:24, :].reshape(PAIRS * 8, 2 * RANK))
    gram = gram * rows_gram(received[:, 24:40, :].reshape(PAIRS * 16, 2 * RANK))
    lane = lax.broadcasted_iota(jnp.int32, (RANK, 2 * RANK), 1)
    row = lax.broadcasted_iota(jnp.int32, (RANK, 2 * RANK), 0)
    whole = jnp.where(lane < RANK, gram, jnp.where(lane == row + RANK, 1.0, 0.0))
    n = RANK // PANEL
    panels = [whole[PANEL * t : PANEL * (t + 1)] for t in range(n)]
    sub = lax.broadcasted_iota(jnp.int32, (PANEL, 2 * RANK), 0)
    for t in range(n):
        panel = panels[t]
        columns = [
            jnp.broadcast_to(panel[:, PANEL * t + j : PANEL * t + j + 1], panel.shape) for j in range(PANEL)
        ]
        inverses = []
        for k in range(PANEL):
            inverses.append(1.0 / columns[k][k : k + 1, :])
            if k == PANEL - 1:
                break
            first = (k + 1) // 8 * 8
            factor = jnp.where(sub[first:] > k, columns[k][first:], 0.0) * inverses[k]

            def eliminate(v):
                low = v[first:] - factor * v[k : k + 1, :]
                return jnp.concatenate([v[:first], low], axis=0) if first else low

            for j in range(k + 1, PANEL):
                columns[j] = eliminate(columns[j])
            panel = eliminate(panel)
        panels[t] = panel
        if t < n - 1:
            factors = jnp.transpose(panel * jnp.concatenate(inverses, axis=0))
            for u in range(t + 1, n):
                rest = panels[u]
                for k in range(PANEL):
                    rest = rest - factors[PANEL * u : PANEL * (u + 1), k : k + 1] * panel[k : k + 1, :]
                panels[u] = rest
    whole = jnp.concatenate(panels, axis=0)
    pivots = jnp.sum(jnp.where(lane == row, whole, 0.0), axis=1, keepdims=True)
    inverse = jnp.where(lane >= RANK, whole * lax.rsqrt(pivots), 0.0)
    out[:RANK, :] = swap_halves(inverse)
    out[RANK:, :] = inverse


def finish_kernel(w0, w1, w2, w3, inverse, out, every, rows):
    z, _, _, _ = place()
    for s, part in enumerate((w0, w1, w2, w3)):
        at = lax.rem(z - s + N_Z, N_Z) * 16
        every[pl.ds(pl.multiple_of(at, 16), 16), :] = part[...]
    inv = inverse[...]
    half = lax.dot_general(every[...], inv, (((1,), (1,)), ((), ())), precision=HIGH, preferred_element_type=jnp.float32)
    solved = jnp.dot(half, inv, precision=HIGH, preferred_element_type=jnp.float32)
    rows[...] = solved
    gram = fold(rows_gram(solved) * (1.0 / I_ALL))
    own = rows[pl.ds(pl.multiple_of(z * 16, 16), 16), :]
    for q in range(ID):
        out[q, : RANK // 2, :] = gram
        for core in range(2):
            row, at = core * 8 + q % 8, RANK // 2 + core * 4
            out[q, at : at + 4, :] = jnp.broadcast_to(own[row : row + 1], (4, 2 * RANK))


def unpack_kernel(received, swapped, rows, gram):
    _, core, x, y = place()
    upper = x * N_KA + y >= 8
    half = RANK // 2

    def unpack(here):
        for p in range(PAIRS):
            for side in range(2):
                source = received if side == here else swapped
                gram[2 * p + side, :half] = source[p, :half, :RANK]
                gram[2 * p + side, half:] = source[p, :half, RANK:]
                row = source[p, half + 4 * here : half + 4 * here + 1, :]
                rows[2 * p + side, 0] = jnp.where(upper, row[:, RANK:], row[:, :RANK])

    for here in range(2):
        pl.when(core == here)(lambda here=here: unpack(here))


LINE = [[(i, (i + s) % 4) for i in range(4)] for s in range(1, 4)]


def around(value, axis):
    return [value] + [lax.ppermute(value, axis, perm) for perm in LINE]


def swap_cores(value):
    return lax.ppermute(value, "core", [(0, 1), (1, 0)])


def on_device(tensor, factor_b, factor_c):
    packed = call(
        pack_kernel,
        f32(PAIRS, 8, 2 * RANK),
        [pltpu.with_memory_space_constraint(f, pltpu.HBM) for f in (factor_b[:, 0], factor_c[:, 0], tensor)],
        specs=[ANY, ANY, ANY],
        scratch=[
            pltpu.VMEM((FIELDS, B_OWN, RANK), jnp.float32),
            pltpu.VMEM((FIELDS, C_OWN, RANK), jnp.float32),
            pltpu.SemaphoreType.DMA((2,)),
        ],
    )
    parts = around(packed, "z")
    near = pltpu.with_memory_space_constraint(tensor, pltpu.VMEM)
    b, c = call(along_z_kernel, (f32(PAIRS, 8, 2 * RANK), f32(PAIRS, 16, 2 * RANK)), parts)
    parts = around(b, "ka") + around(c, "ja")
    mine = call(along_xy_kernel, f32(PAIRS, 96, 2 * RANK), parts)
    other = swap_cores(mine)
    half = pl.CostEstimate(flops=8 * tensor.size * RANK, bytes_accessed=2 * tensor.size, transcendentals=0)
    theirs = call(other_fields_kernel, f32(PAIRS, 8, 2 * RANK), (near, mine, other), vmem=28, cost=half)
    swapped = swap_cores(theirs)
    sums = call(own_fields_kernel, f32(PAIRS, 40, 2 * RANK), (near, mine, other), vmem=28, cost=half)
    sent = call(join_kernel, f32(PAIRS, 40, 2 * RANK), (sums, swapped))
    received = lax.all_to_all(sent, ("ja", "ka"), 0, 0)
    owned = call(total_kernel, f32(16, 2 * RANK), (received,))
    parts = around(owned, "z")
    inverse = call(
        factor_kernel,
        f32(2 * RANK, 2 * RANK),
        (received,),
        cost=pl.CostEstimate(flops=4 * RANK**3, bytes_accessed=10 * MIB, transcendentals=0),
    )
    sent = call(
        finish_kernel,
        f32(PAIRS, RANK // 2 + 8, 2 * RANK),
        (*parts, inverse),
        scratch=[pltpu.VMEM((I_ALL // 2, 2 * RANK), jnp.float32)] * 2,
    )
    received = lax.all_to_all(sent, ("ja", "ka"), 0, 0)
    swapped = swap_cores(received)
    rows, gram = call(unpack_kernel, (f32(FIELDS, 1, 1, RANK), f32(FIELDS, RANK, RANK)), (received, swapped))
    return rows, gram


def solution(mesh):
    return jax.shard_map(
        on_device,
        mesh=Mesh(mesh.devices.reshape(N_Z, 2, N_JA, N_KA), ("z", "core", "ja", "ka")),
        in_specs=(
            P(None, ("z", "core"), "ja", "ka"),
            P(None, "ja", ("z", "core", "ka"), None),
            P(None, "ka", ("z", "core", "ja"), None),
        ),
        out_specs=(P(None, ("z", "core"), ("ja", "ka"), None), P()),
        check_vma=False,
    )
```

```python
import jax
import jax.numpy as jnp
from jax import lax
from jax.experimental import pallas as pl
from jax.experimental.pallas import tpu as pltpu
from jax.sharding import Mesh
from jax.sharding import PartitionSpec as P

FIELDS, RANK = 32, 64
PAIRS = FIELDS // 2
ID, JD, KD = 16, 64, 128
N_IA, N_JA, N_KA = 8, 4, 4
N_Z = N_IA // 2
B_OWN = JD // (N_IA * N_KA)
C_OWN = KD // (N_IA * N_JA)
I_ALL = N_IA * ID
HIGH = lax.Precision.HIGHEST
MIB = 1024 * 1024
VMEM = pl.BlockSpec(memory_space=pltpu.VMEM)
ANY = pl.BlockSpec(memory_space=pl.ANY)
PANEL = 16
UNROLL = 8


def call(kernel, out_shape, operands, *, specs=None, scratch=(), vmem=16, cost=None):
    return pl.pallas_call(
        kernel,
        out_shape=out_shape,
        in_specs=[VMEM] * len(operands) if specs is None else specs,
        out_specs=jax.tree.map(lambda _: VMEM, out_shape),
        scratch_shapes=list(scratch),
        cost_estimate=cost,
        compiler_params=pltpu.CompilerParams(vmem_limit_bytes=vmem * MIB),
    )(*operands)


def f32(*shape):
    return jax.ShapeDtypeStruct(shape, jnp.float32)


def place():
    return tuple(lax.axis_index(axis) for axis in ("z", "core", "ja", "ka"))


def pack_kernel(b_hbm, c_hbm, tensor, out, b, c, sems):
    copies = [pltpu.make_async_copy(b_hbm, b, sems.at[0]), pltpu.make_async_copy(c_hbm, c, sems.at[1])]
    for copy in copies:
        copy.start()
    for copy in copies:
        copy.wait()
    for p in range(PAIRS):
        for side in range(2):
            lanes = slice(side * RANK, (side + 1) * RANK)
            out[p, 0:B_OWN, lanes] = b[2 * p + side]
            out[p, B_OWN : B_OWN + C_OWN, lanes] = c[2 * p + side]
        out[p, B_OWN + C_OWN :, :] = jnp.zeros((8 - B_OWN - C_OWN, 2 * RANK), jnp.float32)


def in_order(pieces, first, rows):
    n = len(pieces)
    rising = jnp.concatenate([pieces[-t % n] for t in range(n)], axis=0)
    return pltpu.roll(rising, first * rows, 0)


def swap_halves(v):
    return pltpu.roll(v, RANK, 1)


def fold(v):
    half = v.shape[0] // 2
    lane = lax.broadcasted_iota(jnp.int32, (1, 2 * RANK), 1)
    return jnp.where(lane < RANK, v[:half], swap_halves(v[half:]))


def along_z_kernel(m0, m1, m2, m3, b, c):
    z, _, _, _ = place()
    parts = (m0, m1, m2, m3)
    for p in range(PAIRS):
        b[p] = in_order([m[p, :B_OWN, :] for m in parts], z, B_OWN)
        c[p] = in_order([m[p, B_OWN : B_OWN + C_OWN, :] for m in parts], z, C_OWN)


def along_xy_kernel(b0, b1, b2, b3, c0, c1, c2, c3, out):
    _, _, x, y = place()
    for p in range(PAIRS):
        for z in range(N_Z):
            rows = slice(z * B_OWN, (z + 1) * B_OWN)
            n = B_OWN * N_KA
            out[p, z * n : (z + 1) * n, :] = in_order([b[p, rows, :] for b in (b0, b1, b2, b3)], y, B_OWN)
        for z in range(N_Z):
            rows = slice(z * C_OWN, (z + 1) * C_OWN)
            n = C_OWN * N_JA
            at = JD // 2 + z * n
            out[p, at : at + n, :] = in_order([c[p, rows, :] for c in (c0, c1, c2, c3)], x, C_OWN)


def contract(p, side, tensor, mine, other):
    first_core = lax.axis_index("core") == 0
    left = lax.broadcasted_iota(jnp.int32, (1, 2 * RANK), 1) < RANK
    nb, nc = B_OWN * N_KA, C_OWN * N_JA

    def both(at, rows):
        here, there = mine[p, at : at + rows, :], other[p, at : at + rows, :]
        return [jnp.where(first_core, here, there), jnp.where(first_core, there, here)]

    def chosen(v):
        return jnp.where(side == 0, v, swap_halves(v))

    b = chosen(jnp.concatenate([part for z in range(N_Z) for part in both(z * nb, nb)], axis=0))
    c = chosen(jnp.concatenate([part for z in range(N_Z) for part in both(JD // 2 + z * nc, nc)], axis=0))
    c1 = c.astype(jnp.bfloat16).astype(jnp.float32)
    c2 = (c - c1).astype(jnp.bfloat16).astype(jnp.float32)
    c3 = c - c1 - c2
    first = jnp.where(left, c1, swap_halves(c2))
    second = jnp.where(left, c3, 0.0)
    weight = jnp.where(left, b, swap_halves(b))
    pieces = jnp.concatenate([first.astype(jnp.bfloat16), second.astype(jnp.bfloat16)], axis=1)
    block = tensor[2 * p + side].reshape(ID * JD, KD)
    high = block.astype(jnp.bfloat16)
    low = (block - high.astype(jnp.float32)).astype(jnp.bfloat16)
    product = jnp.dot(
        jnp.concatenate([high, low], axis=1),
        jnp.concatenate([pieces, pieces], axis=0),
        preferred_element_type=jnp.float32,
    )
    product = (product[:, :KD] + product[:, KD:]).reshape(ID, JD, KD) * weight
    total = jnp.sum(product.reshape(ID, JD // 8, 8, KD).sum(axis=1), axis=1)
    return fold(total + swap_halves(total))


def by_pairs(body):
    def step(n, carry):
        for u in range(UNROLL):
            body(n * UNROLL + u)
        return carry

    lax.fori_loop(0, PAIRS // UNROLL, step, 0)


def other_fields_kernel(tensor, mine, other, out):
    side = 1 - lax.axis_index("core")

    def pair(p):
        out[p] = contract(p, side, tensor, mine, other)

    by_pairs(pair)


def own_fields_kernel(tensor, mine, other, out):
    _, core, x, y = place()
    first_core = core == 0
    nb, nc = B_OWN * N_KA, C_OWN * N_JA

    def share(p, at, rows):
        here, there = mine[p, pl.ds(at, rows), :], other[p, pl.ds(at, rows), :]
        parts = [jnp.where(first_core, here, there), jnp.where(first_core, there, here)]
        part = jnp.concatenate(parts, axis=0)
        return fold(jnp.where(first_core, part, swap_halves(part)))

    def pair(p):
        out[p, pl.ds(pl.multiple_of(8 * (1 - core), 8), 8), :] = jnp.zeros((8, 2 * RANK), jnp.float32)
        out[p, pl.ds(pl.multiple_of(8 * core, 8), 8), :] = contract(p, core, tensor, mine, other)
        out[p, 16:24, :] = share(p, pl.multiple_of(y * nb, nb), nb)
        out[p, 24:40, :] = share(p, pl.multiple_of(JD // 2 + x * nc, nc), nc)

    by_pairs(pair)


def join_kernel(sums, swapped, out):
    at = pl.multiple_of(8 * (1 - lax.axis_index("core")), 8)
    out[...] = sums[...]
    out[:, pl.ds(at, 8), :] = swapped[...]


def total_kernel(received, out):
    total = received[0, :16, :]
    for s in range(1, PAIRS):
        total = total + received[s, :16, :]
    out[...] = total


def rows_gram(rows):
    both = lax.dot_general(rows, rows, (((0,), (0,)), ((), ())), precision=HIGH, preferred_element_type=jnp.float32)
    return both[:RANK] + swap_halves(both[RANK:])


def factor_kernel(received, out):
    gram = rows_gram(received[:, 16:24, :].reshape(PAIRS * 8, 2 * RANK))
    gram = gram * rows_gram(received[:, 24:40, :].reshape(PAIRS * 16, 2 * RANK))
    lane = lax.broadcasted_iota(jnp.int32, (RANK, 2 * RANK), 1)
    row = lax.broadcasted_iota(jnp.int32, (RANK, 2 * RANK), 0)
    whole = jnp.where(lane < RANK, gram, jnp.where(lane == row + RANK, 1.0, 0.0))
    n = RANK // PANEL
    panels = [whole[PANEL * t : PANEL * (t + 1)] for t in range(n)]
    sub = lax.broadcasted_iota(jnp.int32, (PANEL, 2 * RANK), 0)
    for t in range(n):
        panel = panels[t]
        columns = [
            jnp.broadcast_to(panel[:, PANEL * t + j : PANEL * t + j + 1], panel.shape) for j in range(PANEL)
        ]
        inverses = []
        for k in range(PANEL):
            inverses.append(1.0 / columns[k][k : k + 1, :])
            if k == PANEL - 1:
                break
            first = (k + 1) // 8 * 8
            factor = jnp.where(sub[first:] > k, columns[k][first:], 0.0) * inverses[k]

            def eliminate(v):
                low = v[first:] - factor * v[k : k + 1, :]
                return jnp.concatenate([v[:first], low], axis=0) if first else low

            for j in range(k + 1, PANEL):
                columns[j] = eliminate(columns[j])
            panel = eliminate(panel)
        panels[t] = panel
        if t < n - 1:
            factors = jnp.transpose(panel * jnp.concatenate(inverses, axis=0))
            for u in range(t + 1, n):
                rest = panels[u]
                for k in range(PANEL):
                    rest = rest - factors[PANEL * u : PANEL * (u + 1), k : k + 1] * panel[k : k + 1, :]
                panels[u] = rest
    whole = jnp.concatenate(panels, axis=0)
    pivots = jnp.sum(jnp.where(lane == row, whole, 0.0), axis=1, keepdims=True)
    inverse = jnp.where(lane >= RANK, whole * lax.rsqrt(pivots), 0.0)
    twice = jnp.concatenate([swap_halves(inverse), inverse], axis=0)
    out[...] = lax.dot_general(
        twice, twice, (((0,), (0,)), ((), ())), precision=HIGH, preferred_element_type=jnp.float32
    )


def finish_kernel(w0, w1, w2, w3, inverse, out, every, rows):
    z, _, _, _ = place()
    for s, part in enumerate((w0, w1, w2, w3)):
        at = lax.rem(z - s + N_Z, N_Z) * 16
        every[pl.ds(pl.multiple_of(at, 16), 16), :] = part[...]
    solved = jnp.dot(every[...], inverse[...], precision=HIGH, preferred_element_type=jnp.float32)
    rows[...] = solved
    gram = fold(rows_gram(solved) * (1.0 / I_ALL))
    own = rows[pl.ds(pl.multiple_of(z * 16, 16), 16), :]
    for q in range(ID):
        out[q, : RANK // 2, :] = gram
        for core in range(2):
            row, at = core * 8 + q % 8, RANK // 2 + core * 4
            out[q, at : at + 4, :] = jnp.broadcast_to(own[row : row + 1], (4, 2 * RANK))


def unpack_kernel(received, swapped, rows, gram):
    _, core, x, y = place()
    upper = x * N_KA + y >= 8
    half = RANK // 2

    def unpack(here):
        for p in range(PAIRS):
            for side in range(2):
                source = received if side == here else swapped
                gram[2 * p + side, :half] = source[p, :half, :RANK]
                gram[2 * p + side, half:] = source[p, :half, RANK:]
                row = source[p, half + 4 * here : half + 4 * here + 1, :]
                rows[2 * p + side, 0] = jnp.where(upper, row[:, RANK:], row[:, :RANK])

    for here in range(2):
        pl.when(core == here)(lambda here=here: unpack(here))


LINE = [[(i, (i + s) % 4) for i in range(4)] for s in range(1, 4)]


def around(value, axis):
    return [value] + [lax.ppermute(value, axis, perm) for perm in LINE]


def swap_cores(value):
    return lax.ppermute(value, "core", [(0, 1), (1, 0)])


def on_device(tensor, factor_b, factor_c):
    packed = call(
        pack_kernel,
        f32(PAIRS, 8, 2 * RANK),
        [pltpu.with_memory_space_constraint(f, pltpu.HBM) for f in (factor_b[:, 0], factor_c[:, 0], tensor)],
        specs=[ANY, ANY, ANY],
        scratch=[
            pltpu.VMEM((FIELDS, B_OWN, RANK), jnp.float32),
            pltpu.VMEM((FIELDS, C_OWN, RANK), jnp.float32),
            pltpu.SemaphoreType.DMA((2,)),
        ],
    )
    parts = around(packed, "z")
    near = pltpu.with_memory_space_constraint(tensor, pltpu.VMEM)
    b, c = call(along_z_kernel, (f32(PAIRS, 8, 2 * RANK), f32(PAIRS, 16, 2 * RANK)), parts)
    parts = around(b, "ka") + around(c, "ja")
    mine = call(along_xy_kernel, f32(PAIRS, 96, 2 * RANK), parts)
    other = swap_cores(mine)
    half = pl.CostEstimate(flops=8 * tensor.size * RANK, bytes_accessed=2 * tensor.size, transcendentals=0)
    theirs = call(other_fields_kernel, f32(PAIRS, 8, 2 * RANK), (near, mine, other), vmem=28, cost=half)
    swapped = swap_cores(theirs)
    sums = call(own_fields_kernel, f32(PAIRS, 40, 2 * RANK), (near, mine, other), vmem=28, cost=half)
    sent = call(join_kernel, f32(PAIRS, 40, 2 * RANK), (sums, swapped))
    received = lax.all_to_all(sent, ("ja", "ka"), 0, 0)
    owned = call(total_kernel, f32(16, 2 * RANK), (received,))
    parts = around(owned, "z")
    inverse = call(
        factor_kernel,
        f32(2 * RANK, 2 * RANK),
        (received,),
        cost=pl.CostEstimate(flops=4 * RANK**3, bytes_accessed=10 * MIB, transcendentals=0),
    )
    sent = call(
        finish_kernel,
        f32(PAIRS, RANK // 2 + 8, 2 * RANK),
        (*parts, inverse),
        scratch=[pltpu.VMEM((I_ALL // 2, 2 * RANK), jnp.float32)] * 2,
    )
    received = lax.all_to_all(sent, ("ja", "ka"), 0, 0)
    swapped = swap_cores(received)
    rows, gram = call(unpack_kernel, (f32(FIELDS, 1, 1, RANK), f32(FIELDS, RANK, RANK)), (received, swapped))
    return rows, gram


def solution(mesh):
    return jax.shard_map(
        on_device,
        mesh=Mesh(mesh.devices.reshape(N_Z, 2, N_JA, N_KA), ("z", "core", "ja", "ka")),
        in_specs=(
            P(None, ("z", "core"), "ja", "ka"),
            P(None, "ja", ("z", "core", "ka"), None),
            P(None, "ka", ("z", "core", "ja"), None),
        ),
        out_specs=(P(None, ("z", "core"), ("ja", "ka"), None), P()),
        check_vma=False,
    )
```

```python
import jax
import jax.numpy as jnp
from jax import lax
from jax.experimental import pallas as pl
from jax.experimental.pallas import tpu as pltpu
from jax.sharding import Mesh
from jax.sharding import PartitionSpec as P

FIELDS, RANK = 32, 64
PAIRS = FIELDS // 2
ID, JD, KD = 16, 64, 128
N_IA, N_JA, N_KA = 8, 4, 4
N_Z = N_IA // 2
B_OWN = JD // (N_IA * N_KA)
C_OWN = KD // (N_IA * N_JA)
I_ALL = N_IA * ID
HIGH = lax.Precision.HIGHEST
MIB = 1024 * 1024
VMEM = pl.BlockSpec(memory_space=pltpu.VMEM)
ANY = pl.BlockSpec(memory_space=pl.ANY)
STEPS = 2
PANEL = 16
UNROLL = 16


def call(kernel, out_shape, operands, *, specs=None, scratch=(), vmem=16, cost=None):
    return pl.pallas_call(
        kernel,
        out_shape=out_shape,
        in_specs=[VMEM] * len(operands) if specs is None else specs,
        out_specs=jax.tree.map(lambda _: VMEM, out_shape),
        scratch_shapes=list(scratch),
        cost_estimate=cost,
        compiler_params=pltpu.CompilerParams(vmem_limit_bytes=vmem * MIB),
    )(*operands)


def f32(*shape):
    return jax.ShapeDtypeStruct(shape, jnp.float32)


def place():
    return tuple(lax.axis_index(axis) for axis in ("z", "core", "ja", "ka"))


def pack_kernel(b_hbm, c_hbm, tensor, out, b, c, sems):
    copies = [pltpu.make_async_copy(b_hbm, b, sems.at[0]), pltpu.make_async_copy(c_hbm, c, sems.at[1])]
    for copy in copies:
        copy.start()
    for copy in copies:
        copy.wait()
    for p in range(PAIRS):
        for side in range(2):
            lanes = slice(side * RANK, (side + 1) * RANK)
            out[p, 0:B_OWN, lanes] = b[2 * p + side]
            out[p, B_OWN : B_OWN + C_OWN, lanes] = c[2 * p + side]
        out[p, B_OWN + C_OWN :, :] = jnp.zeros((8 - B_OWN - C_OWN, 2 * RANK), jnp.float32)


def in_order(pieces, first, rows):
    n = len(pieces)
    rising = jnp.concatenate([pieces[-t % n] for t in range(n)], axis=0)
    return pltpu.roll(rising, first * rows, 0)


def swap_halves(v):
    return pltpu.roll(v, RANK, 1)


def fold(v):
    half = v.shape[0] // 2
    lane = lax.broadcasted_iota(jnp.int32, (1, 2 * RANK), 1)
    return jnp.where(lane < RANK, v[:half], swap_halves(v[half:]))


def along_z_kernel(m0, m1, m2, m3, b, c):
    z, _, _, _ = place()
    parts = (m0, m1, m2, m3)
    for p in range(PAIRS):
        b[p] = in_order([m[p, :B_OWN, :] for m in parts], z, B_OWN)
        c[p] = in_order([m[p, B_OWN : B_OWN + C_OWN, :] for m in parts], z, C_OWN)


def along_xy_kernel(b0, b1, b2, b3, c0, c1, c2, c3, out):
    _, _, x, y = place()
    for p in range(PAIRS):
        for z in range(N_Z):
            rows = slice(z * B_OWN, (z + 1) * B_OWN)
            n = B_OWN * N_KA
            out[p, z * n : (z + 1) * n, :] = in_order([b[p, rows, :] for b in (b0, b1, b2, b3)], y, B_OWN)
        for z in range(N_Z):
            rows = slice(z * C_OWN, (z + 1) * C_OWN)
            n = C_OWN * N_JA
            at = JD // 2 + z * n
            out[p, at : at + n, :] = in_order([c[p, rows, :] for c in (c0, c1, c2, c3)], x, C_OWN)


def contract(p, side, tensor, mine, other):
    first_core = lax.axis_index("core") == 0
    left = lax.broadcasted_iota(jnp.int32, (1, 2 * RANK), 1) < RANK
    nb, nc = B_OWN * N_KA, C_OWN * N_JA

    def both(at, rows):
        here, there = mine[p, at : at + rows, :], other[p, at : at + rows, :]
        return [jnp.where(first_core, here, there), jnp.where(first_core, there, here)]

    def chosen(v):
        return pltpu.roll(v, RANK * side, 1)

    b = chosen(jnp.concatenate([part for z in range(N_Z) for part in both(z * nb, nb)], axis=0))
    c = chosen(jnp.concatenate([part for z in range(N_Z) for part in both(JD // 2 + z * nc, nc)], axis=0))
    c1 = c.astype(jnp.bfloat16).astype(jnp.float32)
    c2 = (c - c1).astype(jnp.bfloat16).astype(jnp.float32)
    c3 = c - c1 - c2
    first = jnp.where(left, c1, swap_halves(c2))
    second = jnp.where(left, c3, 0.0)
    weight = jnp.where(left, b, swap_halves(b))
    pieces = jnp.concatenate([first.astype(jnp.bfloat16), second.astype(jnp.bfloat16)], axis=1)
    block = tensor[2 * p + side].reshape(ID * JD, KD)
    high = block.astype(jnp.bfloat16)
    low = (block - high.astype(jnp.float32)).astype(jnp.bfloat16)
    product = jnp.dot(
        jnp.concatenate([high, low], axis=1),
        jnp.concatenate([pieces, pieces], axis=0),
        preferred_element_type=jnp.float32,
    )
    product = (product[:, :KD] + product[:, KD:]).reshape(ID, JD, KD) * weight
    total = jnp.sum(product.reshape(ID, JD // 8, 8, KD).sum(axis=1), axis=1)
    return fold(total + swap_halves(total))


def by_pairs(body):
    def step(n, carry):
        for u in range(UNROLL):
            body(n * UNROLL + u)
        return carry

    lax.fori_loop(0, PAIRS // UNROLL, step, 0)


def other_fields_kernel(tensor, mine, other, out):
    side = 1 - lax.axis_index("core")

    def pair(p):
        out[p] = contract(p, side, tensor, mine, other)

    by_pairs(pair)


def own_fields_kernel(tensor, mine, other, out):
    _, core, x, y = place()
    first_core = core == 0
    nb, nc = B_OWN * N_KA, C_OWN * N_JA

    def share(p, at, rows):
        here, there = mine[p, pl.ds(at, rows), :], other[p, pl.ds(at, rows), :]
        parts = [jnp.where(first_core, here, there), jnp.where(first_core, there, here)]
        part = jnp.concatenate(parts, axis=0)
        return fold(jnp.where(first_core, part, swap_halves(part)))

    def pair(p):
        out[p, pl.ds(pl.multiple_of(8 * (1 - core), 8), 8), :] = jnp.zeros((8, 2 * RANK), jnp.float32)
        out[p, pl.ds(pl.multiple_of(8 * core, 8), 8), :] = contract(p, core, tensor, mine, other)
        out[p, 16:24, :] = share(p, pl.multiple_of(y * nb, nb), nb)
        out[p, 24:40, :] = share(p, pl.multiple_of(JD // 2 + x * nc, nc), nc)

    by_pairs(pair)


def join_kernel(sums, swapped, out):
    at = pl.multiple_of(8 * (1 - lax.axis_index("core")), 8)
    out[...] = sums[...]
    out[:, pl.ds(at, 8), :] = swapped[...]


def total_kernel(received, out):
    total = received[0, :16, :]
    for s in range(1, PAIRS):
        total = total + received[s, :16, :]
    out[...] = total


def rows_gram(rows):
    both = lax.dot_general(rows, rows, (((0,), (0,)), ((), ())), precision=HIGH, preferred_element_type=jnp.float32)
    return both[:RANK] + swap_halves(both[RANK:])


def factor_kernel(received, out):
    gram = rows_gram(received[:, 16:24, :].reshape(PAIRS * 8, 2 * RANK))
    gram = gram * rows_gram(received[:, 24:40, :].reshape(PAIRS * 16, 2 * RANK))
    lane = lax.broadcasted_iota(jnp.int32, (RANK, 2 * RANK), 1)
    row = lax.broadcasted_iota(jnp.int32, (RANK, 2 * RANK), 0)
    whole = jnp.where(lane < RANK, gram, jnp.where(lane == row + RANK, 1.0, 0.0))
    n = RANK // PANEL
    panels = [whole[PANEL * t : PANEL * (t + 1)] for t in range(n)]
    sub = lax.broadcasted_iota(jnp.int32, (PANEL, 2 * RANK), 0)
    for t in range(n):
        panel = panels[t]
        columns = [
            jnp.broadcast_to(panel[:, PANEL * t + j : PANEL * t + j + 1], panel.shape) for j in range(PANEL)
        ]
        inverses = []
        for k in range(PANEL):
            inverses.append(1.0 / columns[k][k : k + 1, :])
            if k == PANEL - 1:
                break
            first = (k + 1) // 8 * 8
            factor = jnp.where(sub[first:] > k, columns[k][first:], 0.0) * inverses[k]

            def eliminate(v):
                low = v[first:] - factor * v[k : k + 1, :]
                return jnp.concatenate([v[:first], low], axis=0) if first else low

            for j in range(k + 1, PANEL):
                columns[j] = eliminate(columns[j])
            panel = eliminate(panel)
        panels[t] = panel
        if t < n - 1:
            factors = jnp.transpose(panel * jnp.concatenate(inverses, axis=0))
            for u in range(t + 1, n):
                rest = panels[u]
                for k in range(PANEL):
                    rest = rest - factors[PANEL * u : PANEL * (u + 1), k : k + 1] * panel[k : k + 1, :]
                panels[u] = rest
    whole = jnp.concatenate(panels, axis=0)
    pivots = jnp.sum(jnp.where(lane == row, whole, 0.0), axis=1, keepdims=True)
    inverse = jnp.where(lane >= RANK, whole * lax.rsqrt(pivots), 0.0)
    twice = jnp.concatenate([swap_halves(inverse), inverse], axis=0)
    out[...] = lax.dot_general(
        twice, twice, (((0,), (0,)), ((), ())), precision=HIGH, preferred_element_type=jnp.float32
    )


def finish_kernel(w0, w1, w2, w3, inverse, out, every, rows):
    z, _, _, _ = place()
    for s, part in enumerate((w0, w1, w2, w3)):
        at = lax.rem(z - s + N_Z, N_Z) * 16
        every[pl.ds(pl.multiple_of(at, 16), 16), :] = part[...]
    solved = jnp.dot(every[...], inverse[...], precision=HIGH, preferred_element_type=jnp.float32)
    rows[...] = solved
    gram = fold(rows_gram(solved) * (1.0 / I_ALL))
    own = rows[pl.ds(pl.multiple_of(z * 16, 16), 16), :]
    for q in range(ID):
        out[q, : RANK // 2, :] = gram
        for core in range(2):
            row, at = core * 8 + q % 8, RANK // 2 + core * 4
            out[q, at : at + 4, :] = jnp.broadcast_to(own[row : row + 1], (4, 2 * RANK))


def unpack_kernel(received, swapped, rows, gram):
    _, core, x, y = place()
    upper = x * N_KA + y >= 8
    half = RANK // 2
    first = pl.program_id(0) * (PAIRS // STEPS)

    def unpack(here):
        for n in range(PAIRS // STEPS):
            for side in range(2):
                source = received if side == here else swapped
                gram[2 * n + side, :half] = source[first + n, :half, :RANK]
                gram[2 * n + side, half:] = source[first + n, :half, RANK:]
                row = source[first + n, half + 4 * here : half + 4 * here + 1, :]
                rows[2 * n + side, 0] = jnp.where(upper, row[:, RANK:], row[:, :RANK])

    for here in range(2):
        pl.when(core == here)(lambda here=here: unpack(here))


LINE = [[(i, (i + s) % 4) for i in range(4)] for s in range(1, 4)]


def around(value, axis):
    return [value] + [lax.ppermute(value, axis, perm) for perm in LINE]


def swap_cores(value):
    return lax.ppermute(value, "core", [(0, 1), (1, 0)])


def on_device(tensor, factor_b, factor_c):
    packed = call(
        pack_kernel,
        f32(PAIRS, 8, 2 * RANK),
        [pltpu.with_memory_space_constraint(f, pltpu.HBM) for f in (factor_b[:, 0], factor_c[:, 0], tensor)],
        specs=[ANY, ANY, ANY],
        scratch=[
            pltpu.VMEM((FIELDS, B_OWN, RANK), jnp.float32),
            pltpu.VMEM((FIELDS, C_OWN, RANK), jnp.float32),
            pltpu.SemaphoreType.DMA((2,)),
        ],
    )
    parts = around(packed, "z")
    near = pltpu.with_memory_space_constraint(tensor, pltpu.VMEM)
    b, c = call(along_z_kernel, (f32(PAIRS, 8, 2 * RANK), f32(PAIRS, 16, 2 * RANK)), parts)
    parts = around(b, "ka") + around(c, "ja")
    mine = call(along_xy_kernel, f32(PAIRS, 96, 2 * RANK), parts)
    other = swap_cores(mine)
    half = pl.CostEstimate(flops=8 * tensor.size * RANK, bytes_accessed=2 * tensor.size, transcendentals=0)
    theirs = call(other_fields_kernel, f32(PAIRS, 8, 2 * RANK), (near, mine, other), vmem=28, cost=half)
    swapped = swap_cores(theirs)
    sums = call(own_fields_kernel, f32(PAIRS, 40, 2 * RANK), (near, mine, other), vmem=28, cost=half)
    sent = call(join_kernel, f32(PAIRS, 40, 2 * RANK), (sums, swapped))
    received = lax.all_to_all(sent, ("ja", "ka"), 0, 0)
    owned = call(total_kernel, f32(16, 2 * RANK), (received,))
    parts = around(owned, "z")
    inverse = call(
        factor_kernel,
        f32(2 * RANK, 2 * RANK),
        (received,),
        cost=pl.CostEstimate(flops=4 * RANK**3, bytes_accessed=10 * MIB, transcendentals=0),
    )
    sent = call(
        finish_kernel,
        f32(PAIRS, RANK // 2 + 8, 2 * RANK),
        (*parts, inverse),
        scratch=[pltpu.VMEM((I_ALL // 2, 2 * RANK), jnp.float32)] * 2,
    )
    received = lax.all_to_all(sent, ("ja", "ka"), 0, 0)
    swapped = swap_cores(received)
    n = FIELDS // STEPS
    return pl.pallas_call(
        unpack_kernel,
        out_shape=(f32(FIELDS, 1, 1, RANK), f32(FIELDS, RANK, RANK)),
        grid=(STEPS,),
        in_specs=[VMEM, VMEM],
        out_specs=(
            pl.BlockSpec((n, 1, 1, RANK), lambda i: (i, 0, 0, 0)),
            pl.BlockSpec((n, RANK, RANK), lambda i: (i, 0, 0)),
        ),
        compiler_params=pltpu.CompilerParams(vmem_limit_bytes=16 * MIB),
    )(received, swapped)


def solution(mesh):
    return jax.shard_map(
        on_device,
        mesh=Mesh(mesh.devices.reshape(N_Z, 2, N_JA, N_KA), ("z", "core", "ja", "ka")),
        in_specs=(
            P(None, ("z", "core"), "ja", "ka"),
            P(None, "ja", ("z", "core", "ka"), None),
            P(None, "ka", ("z", "core", "ja"), None),
        ),
        out_specs=(P(None, ("z", "core"), ("ja", "ka"), None), P()),
        check_vma=False,
    )
```

```python
import jax
import jax.numpy as jnp
from jax import lax
from jax.experimental import pallas as pl
from jax.experimental.pallas import tpu as pltpu
from jax.sharding import Mesh
from jax.sharding import PartitionSpec as P

FIELDS, RANK = 32, 64
PAIRS = FIELDS // 2
ID, JD, KD = 16, 64, 128
N_IA, N_JA, N_KA = 8, 4, 4
N_Z = N_IA // 2
B_OWN = JD // (N_IA * N_KA)
C_OWN = KD // (N_IA * N_JA)
I_ALL = N_IA * ID
OWNERS = PAIRS * 2
HIGH = lax.Precision.HIGHEST
MIB = 1024 * 1024
VMEM = pl.BlockSpec(memory_space=pltpu.VMEM)
ANY = pl.BlockSpec(memory_space=pl.ANY)
STEPS = 2
PANEL = 16
UNROLL = 16


def call(kernel, out_shape, operands, *, specs=None, scratch=(), vmem=16, cost=None):
    return pl.pallas_call(
        kernel,
        out_shape=out_shape,
        in_specs=[VMEM] * len(operands) if specs is None else specs,
        out_specs=jax.tree.map(lambda _: VMEM, out_shape),
        scratch_shapes=list(scratch),
        cost_estimate=cost,
        compiler_params=pltpu.CompilerParams(vmem_limit_bytes=vmem * MIB),
    )(*operands)


def f32(*shape):
    return jax.ShapeDtypeStruct(shape, jnp.float32)


def place():
    return tuple(lax.axis_index(axis) for axis in ("z", "core", "ja", "ka"))


def pack_kernel(b_hbm, c_hbm, tensor, out, b, c, sems):
    copies = [pltpu.make_async_copy(b_hbm, b, sems.at[0]), pltpu.make_async_copy(c_hbm, c, sems.at[1])]
    for copy in copies:
        copy.start()
    for copy in copies:
        copy.wait()
    for p in range(PAIRS):
        for side in range(2):
            lanes = slice(side * RANK, (side + 1) * RANK)
            out[p, 0:B_OWN, lanes] = b[2 * p + side]
            out[p, B_OWN : B_OWN + C_OWN, lanes] = c[2 * p + side]
        out[p, B_OWN + C_OWN :, :] = jnp.zeros((8 - B_OWN - C_OWN, 2 * RANK), jnp.float32)


def in_order(pieces, first, rows):
    n = len(pieces)
    rising = jnp.concatenate([pieces[-t % n] for t in range(n)], axis=0)
    return pltpu.roll(rising, first * rows, 0)


def swap_halves(v):
    return pltpu.roll(v, RANK, 1)


def fold(v):
    half = v.shape[0] // 2
    lane = lax.broadcasted_iota(jnp.int32, (1, 2 * RANK), 1)
    return jnp.where(lane < RANK, v[:half], swap_halves(v[half:]))


def along_z_kernel(m0, m1, m2, m3, b, c):
    z, _, _, _ = place()
    parts = (m0, m1, m2, m3)
    for p in range(PAIRS):
        b[p] = in_order([m[p, :B_OWN, :] for m in parts], z, B_OWN)
        c[p] = in_order([m[p, B_OWN : B_OWN + C_OWN, :] for m in parts], z, C_OWN)


def along_xy_kernel(b0, b1, b2, b3, c0, c1, c2, c3, out):
    _, _, x, y = place()
    for p in range(PAIRS):
        for z in range(N_Z):
            rows = slice(z * B_OWN, (z + 1) * B_OWN)
            n = B_OWN * N_KA
            out[p, z * n : (z + 1) * n, :] = in_order([b[p, rows, :] for b in (b0, b1, b2, b3)], y, B_OWN)
        for z in range(N_Z):
            rows = slice(z * C_OWN, (z + 1) * C_OWN)
            n = C_OWN * N_JA
            at = JD // 2 + z * n
            out[p, at : at + n, :] = in_order([c[p, rows, :] for c in (c0, c1, c2, c3)], x, C_OWN)


def mttkrp_kernel(tensor, mine, other, out):
    _, core, x, y = place()
    lane = lax.broadcasted_iota(jnp.int32, (1, 2 * RANK), 1)
    left = lane < RANK
    first_core = core == 0
    nb, nc = B_OWN * N_KA, C_OWN * N_JA

    def both(p, at, rows):
        here, there = mine[p, pl.ds(at, rows), :], other[p, pl.ds(at, rows), :]
        return [jnp.where(first_core, here, there), jnp.where(first_core, there, here)]

    def pair(p):
        b = jnp.concatenate([part for z in range(N_Z) for part in both(p, z * nb, nb)], axis=0)
        c = jnp.concatenate([part for z in range(N_Z) for part in both(p, JD // 2 + z * nc, nc)], axis=0)
        part_b = mine[p, pl.ds(pl.multiple_of(y * nb, nb), nb), :]
        part_c = mine[p, pl.ds(pl.multiple_of(JD // 2 + x * nc, nc), nc), :]
        for side in range(2):
            d = side * PAIRS + p
            out[d, 8:16, :] = fold(swap_halves(part_c) if side else part_c)
            part = fold(swap_halves(part_b) if side else part_b)
            out[d, 16:24, :] = jnp.concatenate([part, jnp.zeros_like(part)], axis=0)
        c1 = c.astype(jnp.bfloat16).astype(jnp.float32)
        c2 = (c - c1).astype(jnp.bfloat16).astype(jnp.float32)
        c3 = c - c1 - c2
        for side in range(2):
            if side == 0:
                first = jnp.where(left, c1, swap_halves(c2))
                second = jnp.where(left, c3, 0.0)
                weight = jnp.where(left, b, swap_halves(b))
            else:
                first = jnp.where(left, swap_halves(c1), c2)
                second = jnp.where(left, swap_halves(c3), 0.0)
                weight = jnp.where(left, swap_halves(b), b)
            pieces = jnp.concatenate([first.astype(jnp.bfloat16), second.astype(jnp.bfloat16)], axis=1)
            block = tensor[2 * p + side].reshape(ID * JD, KD)
            high = block.astype(jnp.bfloat16)
            low = (block - high.astype(jnp.float32)).astype(jnp.bfloat16)
            product = jnp.dot(
                jnp.concatenate([high, low], axis=1),
                jnp.concatenate([pieces, pieces], axis=0),
                preferred_element_type=jnp.float32,
            )
            product = (product[:, :KD] + product[:, KD:]).reshape(ID, JD, KD) * weight
            total = jnp.sum(product.reshape(ID, JD // 8, 8, KD).sum(axis=1), axis=1)
            out[side * PAIRS + p, :8, :] = fold(total + swap_halves(total))

    def step(n, carry):
        for u in range(UNROLL):
            pair(n * UNROLL + u)
        return carry

    lax.fori_loop(0, PAIRS // UNROLL, step, 0)


def total_kernel(received, out):
    for core in range(2):
        total = received[core * PAIRS, :8, :]
        for s in range(1, PAIRS):
            total = total + received[core * PAIRS + s, :8, :]
        out[8 * core : 8 * core + 8, :] = total


def rows_gram(rows):
    both = lax.dot_general(rows, rows, (((0,), (0,)), ((), ())), precision=HIGH, preferred_element_type=jnp.float32)
    return both[:RANK] + swap_halves(both[RANK:])


def factor_kernel(received, out):
    gram = rows_gram(received[:, 16:20, :].reshape(OWNERS * 4, 2 * RANK))
    gram = gram * rows_gram(received[:, 8:16, :].reshape(OWNERS * 8, 2 * RANK))
    lane = lax.broadcasted_iota(jnp.int32, (RANK, 2 * RANK), 1)
    row = lax.broadcasted_iota(jnp.int32, (RANK, 2 * RANK), 0)
    whole = jnp.where(lane < RANK, gram, jnp.where(lane == row + RANK, 1.0, 0.0))
    n = RANK // PANEL
    panels = [whole[PANEL * t : PANEL * (t + 1)] for t in range(n)]
    sub = lax.broadcasted_iota(jnp.int32, (PANEL, 2 * RANK), 0)
    for t in range(n):
        panel = panels[t]
        columns = [
            jnp.broadcast_to(panel[:, PANEL * t + j : PANEL * t + j + 1], panel.shape) for j in range(PANEL)
        ]
        inverses = []
        for k in range(PANEL):
            inverses.append(1.0 / columns[k][k : k + 1, :])
            if k == PANEL - 1:
                break
            first = (k + 1) // 8 * 8
            factor = jnp.where(sub[first:] > k, columns[k][first:], 0.0) * inverses[k]

            def eliminate(v):
                low = v[first:] - factor * v[k : k + 1, :]
                return jnp.concatenate([v[:first], low], axis=0) if first else low

            for j in range(k + 1, PANEL):
                columns[j] = eliminate(columns[j])
            panel = eliminate(panel)
        panels[t] = panel
        if t < n - 1:
            factors = jnp.transpose(panel * jnp.concatenate(inverses, axis=0))
            for u in range(t + 1, n):
                rest = panels[u]
                for k in range(PANEL):
                    rest = rest - factors[PANEL * u : PANEL * (u + 1), k : k + 1] * panel[k : k + 1, :]
                panels[u] = rest
    whole = jnp.concatenate(panels, axis=0)
    pivots = jnp.sum(jnp.where(lane == row, whole, 0.0), axis=1, keepdims=True)
    inverse = jnp.where(lane >= RANK, whole * lax.rsqrt(pivots), 0.0)
    twice = jnp.concatenate([swap_halves(inverse), inverse], axis=0)
    out[...] = lax.dot_general(
        twice, twice, (((0,), (0,)), ((), ())), precision=HIGH, preferred_element_type=jnp.float32
    )


def finish_kernel(w0, w1, w2, w3, inverse, out, every, rows):
    z, _, _, _ = place()
    for s, part in enumerate((w0, w1, w2, w3)):
        at = lax.rem(z - s + N_Z, N_Z) * 16
        every[pl.ds(pl.multiple_of(at, 16), 16), :] = part[...]
    solved = jnp.dot(every[...], inverse[...], precision=HIGH, preferred_element_type=jnp.float32)
    rows[...] = solved
    gram = fold(rows_gram(solved) * (1.0 / I_ALL))
    own = rows[pl.ds(pl.multiple_of(z * 16, 16), 16), :]
    for q in range(ID):
        out[q, : RANK // 2, :] = gram
        for core in range(2):
            row, at = core * 8 + q % 8, RANK // 2 + core * 4
            out[q, at : at + 4, :] = jnp.broadcast_to(own[row : row + 1], (4, 2 * RANK))


def unpack_kernel(received, swapped, rows, gram):
    _, core, x, y = place()
    upper = x * N_KA + y >= 8
    half = RANK // 2
    first = pl.program_id(0) * (PAIRS // STEPS)

    def unpack(here):
        for n in range(PAIRS // STEPS):
            for side in range(2):
                source = received if side == here else swapped
                gram[2 * n + side, :half] = source[first + n, :half, :RANK]
                gram[2 * n + side, half:] = source[first + n, :half, RANK:]
                row = source[first + n, half + 4 * here : half + 4 * here + 1, :]
                rows[2 * n + side, 0] = jnp.where(upper, row[:, RANK:], row[:, :RANK])

    for here in range(2):
        pl.when(core == here)(lambda here=here: unpack(here))


LINE = [[(i, (i + s) % 4) for i in range(4)] for s in range(1, 4)]


def around(value, axis):
    return [value] + [lax.ppermute(value, axis, perm) for perm in LINE]


def swap_cores(value):
    return lax.ppermute(value, "core", [(0, 1), (1, 0)])


def on_device(tensor, factor_b, factor_c):
    packed = call(
        pack_kernel,
        f32(PAIRS, 8, 2 * RANK),
        [pltpu.with_memory_space_constraint(f, pltpu.HBM) for f in (factor_b[:, 0], factor_c[:, 0], tensor)],
        specs=[ANY, ANY, ANY],
        scratch=[
            pltpu.VMEM((FIELDS, B_OWN, RANK), jnp.float32),
            pltpu.VMEM((FIELDS, C_OWN, RANK), jnp.float32),
            pltpu.SemaphoreType.DMA((2,)),
        ],
    )
    parts = around(packed, "z")
    near = pltpu.with_memory_space_constraint(tensor, pltpu.VMEM)
    b, c = call(along_z_kernel, (f32(PAIRS, 8, 2 * RANK), f32(PAIRS, 16, 2 * RANK)), parts)
    parts = around(b, "ka") + around(c, "ja")
    mine = call(along_xy_kernel, f32(PAIRS, 96, 2 * RANK), parts)
    other = swap_cores(mine)
    sent = call(
        mttkrp_kernel,
        f32(OWNERS, 24, 2 * RANK),
        (near, mine, other),
        vmem=28,
        cost=pl.CostEstimate(flops=8 * 2 * tensor.size * RANK, bytes_accessed=4 * tensor.size, transcendentals=0),
    )
    received = lax.all_to_all(sent, ("core", "ja", "ka"), 0, 0)
    owned = call(total_kernel, f32(16, 2 * RANK), (received,))
    parts = around(owned, "z")
    inverse = call(
        factor_kernel,
        f32(2 * RANK, 2 * RANK),
        (received,),
        cost=pl.CostEstimate(flops=4 * RANK**3, bytes_accessed=10 * MIB, transcendentals=0),
    )
    sent = call(
        finish_kernel,
        f32(PAIRS, RANK // 2 + 8, 2 * RANK),
        (*parts, inverse),
        scratch=[pltpu.VMEM((I_ALL // 2, 2 * RANK), jnp.float32)] * 2,
    )
    received = lax.all_to_all(sent, ("ja", "ka"), 0, 0)
    swapped = swap_cores(received)
    n = FIELDS // STEPS
    return pl.pallas_call(
        unpack_kernel,
        out_shape=(f32(FIELDS, 1, 1, RANK), f32(FIELDS, RANK, RANK)),
        grid=(STEPS,),
        in_specs=[VMEM, VMEM],
        out_specs=(
            pl.BlockSpec((n, 1, 1, RANK), lambda i: (i, 0, 0, 0)),
            pl.BlockSpec((n, RANK, RANK), lambda i: (i, 0, 0)),
        ),
        compiler_params=pltpu.CompilerParams(vmem_limit_bytes=16 * MIB),
    )(received, swapped)


def solution(mesh):
    return jax.shard_map(
        on_device,
        mesh=Mesh(mesh.devices.reshape(N_Z, 2, N_JA, N_KA), ("z", "core", "ja", "ka")),
        in_specs=(
            P(None, ("z", "core"), "ja", "ka"),
            P(None, "ja", ("z", "core", "ka"), None),
            P(None, "ka", ("z", "core", "ja"), None),
        ),
        out_specs=(P(None, ("z", "core"), ("ja", "ka"), None), P()),
        check_vma=False,
    )
```

```python
import jax
import jax.numpy as jnp
from jax import lax
from jax.experimental import pallas as pl
from jax.experimental.pallas import tpu as pltpu
from jax.sharding import Mesh
from jax.sharding import PartitionSpec as P

FIELDS, RANK = 32, 64
PAIRS = FIELDS // 2
ID, JD, KD = 16, 64, 128
N_IA, N_JA, N_KA = 8, 4, 4
N_Z = N_IA // 2
B_OWN = JD // (N_IA * N_KA)
C_OWN = KD // (N_IA * N_JA)
I_ALL = N_IA * ID
OWNERS = PAIRS * 2
HIGH = lax.Precision.HIGHEST
MIB = 1024 * 1024
VMEM = pl.BlockSpec(memory_space=pltpu.VMEM)
ANY = pl.BlockSpec(memory_space=pl.ANY)
STEPS = 2
PANEL = 16
UNROLL = 16


def call(kernel, out_shape, operands, *, specs=None, scratch=(), vmem=16, cost=None):
    return pl.pallas_call(
        kernel,
        out_shape=out_shape,
        in_specs=[VMEM] * len(operands) if specs is None else specs,
        out_specs=jax.tree.map(lambda _: VMEM, out_shape),
        scratch_shapes=list(scratch),
        cost_estimate=cost,
        compiler_params=pltpu.CompilerParams(vmem_limit_bytes=vmem * MIB),
    )(*operands)


def f32(*shape):
    return jax.ShapeDtypeStruct(shape, jnp.float32)


def place():
    return tuple(lax.axis_index(axis) for axis in ("z", "core", "ja", "ka"))


def pack_kernel(b_hbm, c_hbm, tensor, out, b, c, sems):
    copies = [pltpu.make_async_copy(b_hbm, b, sems.at[0]), pltpu.make_async_copy(c_hbm, c, sems.at[1])]
    for copy in copies:
        copy.start()
    for copy in copies:
        copy.wait()
    for p in range(PAIRS):
        for side in range(2):
            lanes = slice(side * RANK, (side + 1) * RANK)
            out[p * B_OWN : (p + 1) * B_OWN, lanes] = b[2 * p + side]
            at = PAIRS * B_OWN + p * C_OWN
            out[at : at + C_OWN, lanes] = c[2 * p + side]


def in_order(pieces, first, rows):
    n = len(pieces)
    rising = jnp.concatenate([pieces[-t % n] for t in range(n)], axis=0)
    return pltpu.roll(rising, first * rows, 0)


def swap_halves(v):
    return pltpu.roll(v, RANK, 1)


def fold(v):
    half = v.shape[0] // 2
    lane = lax.broadcasted_iota(jnp.int32, (1, 2 * RANK), 1)
    return jnp.where(lane < RANK, v[:half], swap_halves(v[half:]))


def along_z_kernel(m0, m1, m2, m3, b, c):
    z, _, _, _ = place()
    parts = (m0, m1, m2, m3)
    for p in range(PAIRS):
        b[p] = in_order([m[p * B_OWN : (p + 1) * B_OWN, :] for m in parts], z, B_OWN)
        at = PAIRS * B_OWN + p * C_OWN
        c[p] = in_order([m[at : at + C_OWN, :] for m in parts], z, C_OWN)


def along_xy_kernel(b0, b1, b2, b3, c0, c1, c2, c3, out):
    _, _, x, y = place()
    for p in range(PAIRS):
        for z in range(N_Z):
            rows = slice(z * B_OWN, (z + 1) * B_OWN)
            n = B_OWN * N_KA
            out[p, z * n : (z + 1) * n, :] = in_order([b[p, rows, :] for b in (b0, b1, b2, b3)], y, B_OWN)
        for z in range(N_Z):
            rows = slice(z * C_OWN, (z + 1) * C_OWN)
            n = C_OWN * N_JA
            at = JD // 2 + z * n
            out[p, at : at + n, :] = in_order([c[p, rows, :] for c in (c0, c1, c2, c3)], x, C_OWN)


def mttkrp_kernel(tensor, mine, other, out):
    _, core, x, y = place()
    lane = lax.broadcasted_iota(jnp.int32, (1, 2 * RANK), 1)
    left = lane < RANK
    first_core = core == 0
    nb, nc = B_OWN * N_KA, C_OWN * N_JA

    def both(p, at, rows):
        here, there = mine[p, pl.ds(at, rows), :], other[p, pl.ds(at, rows), :]
        return [jnp.where(first_core, here, there), jnp.where(first_core, there, here)]

    def pair(p):
        b = jnp.concatenate([part for z in range(N_Z) for part in both(p, z * nb, nb)], axis=0)
        c = jnp.concatenate([part for z in range(N_Z) for part in both(p, JD // 2 + z * nc, nc)], axis=0)
        part_b = mine[p, pl.ds(pl.multiple_of(y * nb, nb), nb), :]
        part_c = mine[p, pl.ds(pl.multiple_of(JD // 2 + x * nc, nc), nc), :]
        for side in range(2):
            d = 2 * p + side
            out[d, 8:16, :] = fold(swap_halves(part_c) if side else part_c)
            part = fold(swap_halves(part_b) if side else part_b)
            out[d, 16:24, :] = jnp.concatenate([part, jnp.zeros_like(part)], axis=0)
        c1 = c.astype(jnp.bfloat16).astype(jnp.float32)
        c2 = (c - c1).astype(jnp.bfloat16).astype(jnp.float32)
        c3 = c - c1 - c2
        for side in range(2):
            if side == 0:
                first = jnp.where(left, c1, swap_halves(c2))
                second = jnp.where(left, c3, 0.0)
                weight = jnp.where(left, b, swap_halves(b))
            else:
                first = jnp.where(left, swap_halves(c1), c2)
                second = jnp.where(left, swap_halves(c3), 0.0)
                weight = jnp.where(left, swap_halves(b), b)
            pieces = jnp.concatenate([first.astype(jnp.bfloat16), second.astype(jnp.bfloat16)], axis=1)
            block = tensor[2 * p + side].reshape(ID * JD, KD)
            high = block.astype(jnp.bfloat16)
            low = (block - high.astype(jnp.float32)).astype(jnp.bfloat16)
            product = jnp.dot(
                jnp.concatenate([high, low], axis=1),
                jnp.concatenate([pieces, pieces], axis=0),
                preferred_element_type=jnp.float32,
            )
            product = (product[:, :KD] + product[:, KD:]).reshape(ID, JD, KD) * weight
            total = jnp.sum(product.reshape(ID, JD // 8, 8, KD).sum(axis=1), axis=1)
            out[2 * p + side, :8, :] = fold(total + swap_halves(total))

    def step(n, carry):
        for u in range(UNROLL):
            pair(n * UNROLL + u)
        return carry

    lax.fori_loop(0, PAIRS // UNROLL, step, 0)


def total_kernel(received, out):
    for core in range(2):
        total = received[core, :8, :]
        for s in range(1, PAIRS):
            total = total + received[2 * s + core, :8, :]
        out[8 * core : 8 * core + 8, :] = total


def rows_gram(rows):
    both = lax.dot_general(rows, rows, (((0,), (0,)), ((), ())), precision=HIGH, preferred_element_type=jnp.float32)
    return both[:RANK] + swap_halves(both[RANK:])


def factor_kernel(received, out):
    gram = rows_gram(received[:, 16:20, :].reshape(OWNERS * 4, 2 * RANK))
    gram = gram * rows_gram(received[:, 8:16, :].reshape(OWNERS * 8, 2 * RANK))
    lane = lax.broadcasted_iota(jnp.int32, (RANK, 2 * RANK), 1)
    row = lax.broadcasted_iota(jnp.int32, (RANK, 2 * RANK), 0)
    whole = jnp.where(lane < RANK, gram, jnp.where(lane == row + RANK, 1.0, 0.0))
    n = RANK // PANEL
    panels = [whole[PANEL * t : PANEL * (t + 1)] for t in range(n)]
    sub = lax.broadcasted_iota(jnp.int32, (PANEL, 2 * RANK), 0)
    for t in range(n):
        panel = panels[t]
        columns = [
            jnp.broadcast_to(panel[:, PANEL * t + j : PANEL * t + j + 1], panel.shape) for j in range(PANEL)
        ]
        inverses = []
        for k in range(PANEL):
            inverses.append(1.0 / columns[k][k : k + 1, :])
            if k == PANEL - 1:
                break
            first = (k + 1) // 8 * 8
            factor = jnp.where(sub[first:] > k, columns[k][first:], 0.0) * inverses[k]

            def eliminate(v):
                low = v[first:] - factor * v[k : k + 1, :]
                return jnp.concatenate([v[:first], low], axis=0) if first else low

            for j in range(k + 1, PANEL):
                columns[j] = eliminate(columns[j])
            panel = eliminate(panel)
        panels[t] = panel
        if t < n - 1:
            factors = jnp.transpose(panel * jnp.concatenate(inverses, axis=0))
            for u in range(t + 1, n):
                rest = panels[u]
                for k in range(PANEL):
                    rest = rest - factors[PANEL * u : PANEL * (u + 1), k : k + 1] * panel[k : k + 1, :]
                panels[u] = rest
    whole = jnp.concatenate(panels, axis=0)
    pivots = jnp.sum(jnp.where(lane == row, whole, 0.0), axis=1, keepdims=True)
    inverse = jnp.where(lane >= RANK, whole * lax.rsqrt(pivots), 0.0)
    twice = jnp.concatenate([swap_halves(inverse), inverse], axis=0)
    out[...] = lax.dot_general(
        twice, twice, (((0,), (0,)), ((), ())), precision=HIGH, preferred_element_type=jnp.float32
    )


def finish_kernel(w0, w1, w2, w3, inverse, out, every, rows):
    z, _, _, _ = place()
    for s, part in enumerate((w0, w1, w2, w3)):
        at = lax.rem(z - s + N_Z, N_Z) * 16
        every[pl.ds(pl.multiple_of(at, 16), 16), :] = part[...]
    solved = jnp.dot(every[...], inverse[...], precision=HIGH, preferred_element_type=jnp.float32)
    rows[...] = solved
    gram = fold(rows_gram(solved) * (1.0 / I_ALL))
    own = rows[pl.ds(pl.multiple_of(z * 16, 16), 16), :]
    for q in range(ID):
        out[q, : RANK // 2, :] = gram
        for core in range(2):
            row, at = core * 8 + q % 8, RANK // 2 + core * 4
            out[q, at : at + 4, :] = jnp.broadcast_to(own[row : row + 1], (4, 2 * RANK))


def unpack_kernel(received, swapped, rows, gram):
    _, core, x, y = place()
    upper = x * N_KA + y >= 8
    half = RANK // 2
    first = pl.program_id(0) * (PAIRS // STEPS)

    def unpack(here):
        for n in range(PAIRS // STEPS):
            for side in range(2):
                source = received if side == here else swapped
                gram[2 * n + side, :half] = source[first + n, :half, :RANK]
                gram[2 * n + side, half:] = source[first + n, :half, RANK:]
                row = source[first + n, half + 4 * here : half + 4 * here + 1, :]
                rows[2 * n + side, 0] = jnp.where(upper, row[:, RANK:], row[:, :RANK])

    for here in range(2):
        pl.when(core == here)(lambda here=here: unpack(here))


LINE = [[(i, (i + s) % 4) for i in range(4)] for s in range(1, 4)]


def around(value, axis):
    return [value] + [lax.ppermute(value, axis, perm) for perm in LINE]


def swap_cores(value):
    return lax.ppermute(value, "core", [(0, 1), (1, 0)])


def on_device(tensor, factor_b, factor_c):
    packed = call(
        pack_kernel,
        f32(PAIRS * (B_OWN + C_OWN), 2 * RANK),
        [pltpu.with_memory_space_constraint(f, pltpu.HBM) for f in (factor_b[:, 0], factor_c[:, 0], tensor)],
        specs=[ANY, ANY, ANY],
        scratch=[
            pltpu.VMEM((FIELDS, B_OWN, RANK), jnp.float32),
            pltpu.VMEM((FIELDS, C_OWN, RANK), jnp.float32),
            pltpu.SemaphoreType.DMA((2,)),
        ],
    )
    parts = around(packed, "z")
    near = pltpu.with_memory_space_constraint(tensor, pltpu.VMEM)
    b, c = call(along_z_kernel, (f32(PAIRS, 8, 2 * RANK), f32(PAIRS, 16, 2 * RANK)), parts)
    parts = around(b, "ka") + around(c, "ja")
    mine = call(along_xy_kernel, f32(PAIRS, 96, 2 * RANK), parts)
    other = swap_cores(mine)
    sent = call(
        mttkrp_kernel,
        f32(OWNERS, 24, 2 * RANK),
        (near, mine, other),
        vmem=28,
        cost=pl.CostEstimate(flops=8 * 2 * tensor.size * RANK, bytes_accessed=4 * tensor.size, transcendentals=0),
    )
    received = lax.all_to_all(sent, ("ja", "ka", "core"), 0, 0)
    owned = call(total_kernel, f32(16, 2 * RANK), (received,))
    parts = around(owned, "z")
    inverse = call(
        factor_kernel,
        f32(2 * RANK, 2 * RANK),
        (received,),
        cost=pl.CostEstimate(flops=4 * RANK**3, bytes_accessed=10 * MIB, transcendentals=0),
    )
    sent = call(
        finish_kernel,
        f32(PAIRS, RANK // 2 + 8, 2 * RANK),
        (*parts, inverse),
        scratch=[pltpu.VMEM((I_ALL // 2, 2 * RANK), jnp.float32)] * 2,
    )
    received = lax.all_to_all(sent, ("ja", "ka"), 0, 0)
    swapped = swap_cores(received)
    n = FIELDS // STEPS
    return pl.pallas_call(
        unpack_kernel,
        out_shape=(f32(FIELDS, 1, 1, RANK), f32(FIELDS, RANK, RANK)),
        grid=(STEPS,),
        in_specs=[VMEM, VMEM],
        out_specs=(
            pl.BlockSpec((n, 1, 1, RANK), lambda i: (i, 0, 0, 0)),
            pl.BlockSpec((n, RANK, RANK), lambda i: (i, 0, 0)),
        ),
        compiler_params=pltpu.CompilerParams(vmem_limit_bytes=16 * MIB),
    )(received, swapped)


def solution(mesh):
    return jax.shard_map(
        on_device,
        mesh=Mesh(mesh.devices.reshape(N_Z, 2, N_JA, N_KA), ("z", "core", "ja", "ka")),
        in_specs=(
            P(None, ("z", "core"), "ja", "ka"),
            P(None, "ja", ("z", "core", "ka"), None),
            P(None, "ka", ("z", "core", "ja"), None),
        ),
        out_specs=(P(None, ("z", "core"), ("ja", "ka"), None), P()),
        check_vma=False,
    )
```

```python
import jax
import jax.numpy as jnp
from jax import lax
from jax.experimental import pallas as pl
from jax.experimental.pallas import tpu as pltpu
from jax.sharding import Mesh
from jax.sharding import PartitionSpec as P

FIELDS, RANK = 32, 64
PAIRS = FIELDS // 2
ID, JD, KD = 16, 64, 128
N_IA, N_JA, N_KA = 8, 4, 4
N_Z = N_IA // 2
B_OWN = JD // (N_IA * N_KA)
C_OWN = KD // (N_IA * N_JA)
I_ALL = N_IA * ID
OWNERS = PAIRS * 2
HIGH = lax.Precision.HIGHEST
MIB = 1024 * 1024
VMEM = pl.BlockSpec(memory_space=pltpu.VMEM)
ANY = pl.BlockSpec(memory_space=pl.ANY)
STEPS = 2
PANEL = 16
UNROLL = 16


def call(kernel, out_shape, operands, *, specs=None, scratch=(), vmem=16, cost=None):
    return pl.pallas_call(
        kernel,
        out_shape=out_shape,
        in_specs=[VMEM] * len(operands) if specs is None else specs,
        out_specs=jax.tree.map(lambda _: VMEM, out_shape),
        scratch_shapes=list(scratch),
        cost_estimate=cost,
        compiler_params=pltpu.CompilerParams(vmem_limit_bytes=vmem * MIB),
    )(*operands)


def f32(*shape):
    return jax.ShapeDtypeStruct(shape, jnp.float32)


def place():
    return tuple(lax.axis_index(axis) for axis in ("z", "core", "ja", "ka"))


def pack_kernel(b_hbm, c_hbm, tensor, out, b, c, sems):
    copies = [pltpu.make_async_copy(b_hbm, b, sems.at[0]), pltpu.make_async_copy(c_hbm, c, sems.at[1])]
    for copy in copies:
        copy.start()
    for copy in copies:
        copy.wait()
    for p in range(PAIRS):
        for side in range(2):
            lanes = slice(side * RANK, (side + 1) * RANK)
            out[p * B_OWN : (p + 1) * B_OWN, lanes] = b[2 * p + side]
            at = PAIRS * B_OWN + p * C_OWN
            out[at : at + C_OWN, lanes] = c[2 * p + side]


def in_order(pieces, first, rows):
    n = len(pieces)
    rising = jnp.concatenate([pieces[-t % n] for t in range(n)], axis=0)
    return pltpu.roll(rising, first * rows, 0)


def swap_halves(v):
    return pltpu.roll(v, RANK, 1)


def fold(v):
    half = v.shape[0] // 2
    lane = lax.broadcasted_iota(jnp.int32, (1, 2 * RANK), 1)
    return jnp.where(lane < RANK, v[:half], swap_halves(v[half:]))


def along_z_kernel(m0, m1, m2, m3, b, c):
    z, _, _, _ = place()
    parts = (m0, m1, m2, m3)
    for p in range(PAIRS):
        b[p] = in_order([m[p * B_OWN : (p + 1) * B_OWN, :] for m in parts], z, B_OWN)
        at = PAIRS * B_OWN + p * C_OWN
        c[p] = in_order([m[at : at + C_OWN, :] for m in parts], z, C_OWN)


def along_xy_kernel(b0, b1, b2, b3, c0, c1, c2, c3, out):
    _, _, x, y = place()
    for p in range(PAIRS):
        for z in range(N_Z):
            rows = slice(z * B_OWN, (z + 1) * B_OWN)
            n = B_OWN * N_KA
            out[p, z * n : (z + 1) * n, :] = in_order([b[p, rows, :] for b in (b0, b1, b2, b3)], y, B_OWN)
        for z in range(N_Z):
            rows = slice(z * C_OWN, (z + 1) * C_OWN)
            n = C_OWN * N_JA
            at = JD // 2 + z * n
            out[p, at : at + n, :] = in_order([c[p, rows, :] for c in (c0, c1, c2, c3)], x, C_OWN)


def mttkrp_kernel(tensor, mine, other, out):
    _, core, x, y = place()
    lane = lax.broadcasted_iota(jnp.int32, (1, 2 * RANK), 1)
    left = lane < RANK
    first_core = core == 0
    nb, nc = B_OWN * N_KA, C_OWN * N_JA

    def both(p, at, rows):
        here, there = mine[p, pl.ds(at, rows), :], other[p, pl.ds(at, rows), :]
        return [jnp.where(first_core, here, there), jnp.where(first_core, there, here)]

    def pair(p):
        b = jnp.concatenate([part for z in range(N_Z) for part in both(p, z * nb, nb)], axis=0)
        c = jnp.concatenate([part for z in range(N_Z) for part in both(p, JD // 2 + z * nc, nc)], axis=0)
        part_b = mine[p, pl.ds(pl.multiple_of(y * nb, nb), nb), :]
        part_c = mine[p, pl.ds(pl.multiple_of(JD // 2 + x * nc, nc), nc), :]
        for side in range(2):
            d = 2 * p + side
            out[d, 8:16, :] = fold(swap_halves(part_c) if side else part_c)
            part = fold(swap_halves(part_b) if side else part_b)
            out[d, 16:24, :] = jnp.concatenate([part, jnp.zeros_like(part)], axis=0)
        c1 = c.astype(jnp.bfloat16).astype(jnp.float32)
        c2 = (c - c1).astype(jnp.bfloat16).astype(jnp.float32)
        c3 = c - c1 - c2
        for side in range(2):
            if side == 0:
                first = jnp.where(left, c1, swap_halves(c2))
                second = jnp.where(left, c3, 0.0)
                weight = jnp.where(left, b, swap_halves(b))
            else:
                first = jnp.where(left, swap_halves(c1), c2)
                second = jnp.where(left, swap_halves(c3), 0.0)
                weight = jnp.where(left, swap_halves(b), b)
            pieces = jnp.concatenate([first.astype(jnp.bfloat16), second.astype(jnp.bfloat16)], axis=1)
            block = tensor[2 * p + side].reshape(ID * JD, KD)
            high = block.astype(jnp.bfloat16)
            low = (block - high.astype(jnp.float32)).astype(jnp.bfloat16)
            product = jnp.dot(
                jnp.concatenate([high, low], axis=1),
                jnp.concatenate([pieces, pieces], axis=0),
                preferred_element_type=jnp.float32,
            )
            product = (product[:, :KD] + product[:, KD:]).reshape(ID, JD, KD) * weight
            total = jnp.sum(product.reshape(ID, JD // 8, 8, KD).sum(axis=1), axis=1)
            out[2 * p + side, :8, :] = fold(total + swap_halves(total))

    def step(n, carry):
        for u in range(UNROLL):
            pair(n * UNROLL + u)
        return carry

    lax.fori_loop(0, PAIRS // UNROLL, step, 0)


def total_kernel(received, out):
    for core in range(2):
        total = received[core, :8, :]
        for s in range(1, PAIRS):
            total = total + received[2 * s + core, :8, :]
        out[8 * core : 8 * core + 8, :] = total


def rows_gram(rows):
    both = lax.dot_general(rows, rows, (((0,), (0,)), ((), ())), precision=HIGH, preferred_element_type=jnp.float32)
    return both[:RANK] + swap_halves(both[RANK:])


def factor_kernel(received, out):
    gram = rows_gram(received[:, 16:20, :].reshape(OWNERS * 4, 2 * RANK))
    gram = gram * rows_gram(received[:, 8:16, :].reshape(OWNERS * 8, 2 * RANK))
    lane = lax.broadcasted_iota(jnp.int32, (RANK, 2 * RANK), 1)
    row = lax.broadcasted_iota(jnp.int32, (RANK, 2 * RANK), 0)
    whole = jnp.where(lane < RANK, gram, jnp.where(lane == row + RANK, 1.0, 0.0))
    n = RANK // PANEL
    panels = [whole[PANEL * t : PANEL * (t + 1)] for t in range(n)]
    sub = lax.broadcasted_iota(jnp.int32, (PANEL, 2 * RANK), 0)
    for t in range(n):
        panel = panels[t]
        columns = [
            jnp.broadcast_to(panel[:, PANEL * t + j : PANEL * t + j + 1], panel.shape) for j in range(PANEL)
        ]
        inverses = []
        for k in range(PANEL):
            inverses.append(1.0 / columns[k][k : k + 1, :])
            if k == PANEL - 1:
                break
            first = (k + 1) // 8 * 8
            factor = jnp.where(sub[first:] > k, columns[k][first:], 0.0) * inverses[k]

            def eliminate(v):
                low = v[first:] - factor * v[k : k + 1, :]
                return jnp.concatenate([v[:first], low], axis=0) if first else low

            for j in range(k + 1, PANEL):
                columns[j] = eliminate(columns[j])
            panel = eliminate(panel)
        panels[t] = panel
        if t < n - 1:
            factors = jnp.transpose(panel * jnp.concatenate(inverses, axis=0))
            for u in range(t + 1, n):
                rest = panels[u]
                for k in range(PANEL):
                    rest = rest - factors[PANEL * u : PANEL * (u + 1), k : k + 1] * panel[k : k + 1, :]
                panels[u] = rest
    whole = jnp.concatenate(panels, axis=0)
    pivots = jnp.sum(jnp.where(lane == row, whole, 0.0), axis=1, keepdims=True)
    inverse = jnp.where(lane >= RANK, whole * lax.rsqrt(pivots), 0.0)
    twice = jnp.concatenate([swap_halves(inverse), inverse], axis=0)
    out[...] = lax.dot_general(
        twice, twice, (((0,), (0,)), ((), ())), precision=HIGH, preferred_element_type=jnp.float32
    )


def finish_kernel(w0, w1, w2, w3, inverse, out, every, rows):
    z, _, _, _ = place()
    for s, part in enumerate((w0, w1, w2, w3)):
        at = lax.rem(z - s + N_Z, N_Z) * 16
        every[pl.ds(pl.multiple_of(at, 16), 16), :] = part[...]
    solved = jnp.dot(every[...], inverse[...], precision=HIGH, preferred_element_type=jnp.float32)
    rows[...] = solved
    gram = fold(rows_gram(solved) * (1.0 / I_ALL))
    own = rows[pl.ds(pl.multiple_of(z * 16, 16), 16), :]
    for q in range(ID):
        d = q % N_KA * N_JA + q // N_KA
        out[d, : RANK // 2, :] = gram
        for core in range(2):
            row, at = core * 8 + q % 8, RANK // 2 + core * 4
            out[d, at : at + 4, :] = jnp.broadcast_to(own[row : row + 1], (4, 2 * RANK))


def unpack_kernel(received, swapped, rows, gram):
    _, core, x, y = place()
    upper = x * N_KA + y >= 8
    half = RANK // 2
    first = pl.program_id(0) * (PAIRS // STEPS)

    def unpack(here):
        for n in range(PAIRS // STEPS):
            at = n % N_KA * N_JA + first // N_KA + n // N_KA
            for side in range(2):
                source = received if side == here else swapped
                gram[2 * n + side, :half] = source[at, :half, :RANK]
                gram[2 * n + side, half:] = source[at, :half, RANK:]
                row = source[at, half + 4 * here : half + 4 * here + 1, :]
                rows[2 * n + side, 0] = jnp.where(upper, row[:, RANK:], row[:, :RANK])

    for here in range(2):
        pl.when(core == here)(lambda here=here: unpack(here))


LINE = [[(i, (i + s) % 4) for i in range(4)] for s in range(1, 4)]


def around(value, axis):
    return [value] + [lax.ppermute(value, axis, perm) for perm in LINE]


def swap_cores(value):
    return lax.ppermute(value, "core", [(0, 1), (1, 0)])


def on_device(tensor, factor_b, factor_c):
    packed = call(
        pack_kernel,
        f32(PAIRS * (B_OWN + C_OWN), 2 * RANK),
        [pltpu.with_memory_space_constraint(f, pltpu.HBM) for f in (factor_b[:, 0], factor_c[:, 0], tensor)],
        specs=[ANY, ANY, ANY],
        scratch=[
            pltpu.VMEM((FIELDS, B_OWN, RANK), jnp.float32),
            pltpu.VMEM((FIELDS, C_OWN, RANK), jnp.float32),
            pltpu.SemaphoreType.DMA((2,)),
        ],
    )
    parts = around(packed, "z")
    near = pltpu.with_memory_space_constraint(tensor, pltpu.VMEM)
    b, c = call(along_z_kernel, (f32(PAIRS, 8, 2 * RANK), f32(PAIRS, 16, 2 * RANK)), parts)
    parts = around(b, "ka") + around(c, "ja")
    mine = call(along_xy_kernel, f32(PAIRS, 96, 2 * RANK), parts)
    other = swap_cores(mine)
    sent = call(
        mttkrp_kernel,
        f32(OWNERS, 24, 2 * RANK),
        (near, mine, other),
        vmem=28,
        cost=pl.CostEstimate(flops=8 * 2 * tensor.size * RANK, bytes_accessed=4 * tensor.size, transcendentals=0),
    )
    received = lax.all_to_all(sent, ("ja", "ka", "core"), 0, 0)
    owned = call(total_kernel, f32(16, 2 * RANK), (received,))
    parts = around(owned, "z")
    inverse = call(
        factor_kernel,
        f32(2 * RANK, 2 * RANK),
        (received,),
        cost=pl.CostEstimate(flops=4 * RANK**3, bytes_accessed=10 * MIB, transcendentals=0),
    )
    sent = call(
        finish_kernel,
        f32(PAIRS, RANK // 2 + 8, 2 * RANK),
        (*parts, inverse),
        scratch=[pltpu.VMEM((I_ALL // 2, 2 * RANK), jnp.float32)] * 2,
    )
    received = lax.all_to_all(sent, ("ka", "ja"), 0, 0)
    swapped = swap_cores(received)
    n = FIELDS // STEPS
    return pl.pallas_call(
        unpack_kernel,
        out_shape=(f32(FIELDS, 1, 1, RANK), f32(FIELDS, RANK, RANK)),
        grid=(STEPS,),
        in_specs=[VMEM, VMEM],
        out_specs=(
            pl.BlockSpec((n, 1, 1, RANK), lambda i: (i, 0, 0, 0)),
            pl.BlockSpec((n, RANK, RANK), lambda i: (i, 0, 0)),
        ),
        compiler_params=pltpu.CompilerParams(vmem_limit_bytes=16 * MIB),
    )(received, swapped)


def solution(mesh):
    return jax.shard_map(
        on_device,
        mesh=Mesh(mesh.devices.reshape(N_Z, 2, N_JA, N_KA), ("z", "core", "ja", "ka")),
        in_specs=(
            P(None, ("z", "core"), "ja", "ka"),
            P(None, "ja", ("z", "core", "ka"), None),
            P(None, "ka", ("z", "core", "ja"), None),
        ),
        out_specs=(P(None, ("z", "core"), ("ja", "ka"), None), P()),
        check_vma=False,
    )
```
